512 devices in a mesh: blk: 32 (over y, x_lo, core), head: 16 (over z, x_hi).
Axes of the slice: x: 4 (x_hi: 2, x_lo: 2; x = x_hi * 2 + x_lo), y: 8, z: 8, core: 2. Of those that a mesh axis runs over, the one named last changes fastest.
Arguments:
- tokens: bfloat16 [8, 4096, 768], P(None, ('blk', 'head')), may hold values from -6 to 6
- chain_id: int32 [4096], P(('blk', 'head')), may hold values from 0 to 3, never falling along the last dimension, each value on 1 to 2048 neighbouring positions
- hotspots: int32 [16], replicated, may hold values from 0 to 4095
- chain_embed: bfloat16 [4, 768], replicated, may hold values from -6 to 6
- hot_embed: bfloat16 [768], replicated, may hold values from -6 to 6
- w_proj: bfloat16 [768, 3072], P(None, 'head'), may hold values from -0.21875 to 0.21875
- pair_bias: bfloat16 [16, 4096, 4096], P('head', 'blk'), may hold values from -400 to 400
- w_out: bfloat16 [768, 768], P('head'), may hold values from -0.21875 to 0.21875
Outputs:
- update: bfloat16 [8, 4096, 768], P(None, ('blk', 'head'))
The draws below stay inside these ranges and needn't reach their ends.
Inputs may be any that keep to these rules, and one draw needn't show every extreme that they name: `chain_id`: chain ids never fall along the tokens; one chain has exactly 2048 tokens. `hotspots`: positions may repeat.
All inputs are finite; a program needn't handle non-finite values.
Results may differ from the reference program's by a relative error of at most 0.02.
Values may be sent and summed in bfloat16 or wider, within the bound.
No kernel may reach another device: no remote copies, remote signals or barrier semaphores. Data moves between devices by JAX's collectives and lax.ppermute only.
A program may use at most 64 MiB of HBM per device.

```python
import math
import jax
import jax.numpy as jnp
import numpy as np
from jax import lax

D = 768
H = 16
HD = 48
SAMPLES = 8
CHAINS = 4
HOT = 16
N = 4096


def draw_pair_bias(key, part):
    key = jax.random.fold_in(key, 11)
    row_key, col_key, base_key = jax.random.split(key, 3)
    row_scale = jnp.exp(jax.random.uniform(row_key, (H, N, 1), jnp.float32, jnp.log(0.5), jnp.log(1.5)))
    col_scale = jnp.exp(jax.random.uniform(col_key, (H, 1, N), jnp.float32, jnp.log(0.3), jnp.log(3.0)))

    def one_head(inputs):
        head_index, row_part, col_part = inputs
        head_key = jax.random.fold_in(base_key, head_index)
        return jax.random.normal(head_key, (N, N), jnp.float32) * row_part * col_part
    full = lax.map(one_head, (jnp.arange(H, dtype=jnp.int32), row_scale, col_scale))
    return full.astype(jnp.bfloat16)


def touch_ends(values, key, least, top_value):
    dims = values.shape
    place = [jax.random.randint(jax.random.fold_in(key, axis), (), 0, dims[axis]) for axis in range(len(dims))]
    values = values.at[tuple(place)].set(least)
    longest = dims.index(max(dims))
    place[longest] = (place[longest] + 1) % dims[longest]
    return values.at[tuple(place)].set(top_value)


def shard_levels(key, shape, cuts, least, largest):
    def one(axis_at, shards_of):
        heights = jax.random.uniform(jax.random.fold_in(jax.random.fold_in(key, 6), axis_at), (shards_of,), jnp.float32, least / len(cuts), largest / len(cuts))
        return jnp.repeat(jnp.exp(heights), shape[axis_at] // shards_of).reshape((-1,) + (1,) * (len(shape) - axis_at - 1))

    level = one(*cuts[0])
    for cut in cuts[1:]:
        level = level * one(*cut)
    return level


def profile(amount, total, limit, slope):
    loads = [(1 << 20) // math.isqrt(grade ** slope) + 1 for grade in range(2, amount + 1)]
    surplus, given = total - limit - (amount - 1), [1] * (amount - 1)
    while surplus > 0:
        free = [i for i in range(amount - 1) if given[i] < limit]
        pool, remaining = sum([loads[i] for i in free]), surplus
        for i in free:
            more = min(limit - given[i], max(1, remaining * loads[i] // pool), surplus)
            given[i] = given[i] + more
            surplus = surplus - more
    return np.array([limit] + given)


def ragged_sizes(own_key, amount, total, reach, lean):
    if amount == 2:
        one = jax.random.randint(own_key, (), max(1, total - reach), min(reach, total - 1) + 1)
        return jnp.stack([one, total - one])
    tallies = jnp.asarray(profile(amount, total, reach, lean), jnp.int32)
    couples = (amount - 1) // 2
    source_of, receiver = tallies[1:1 + 2 * couples:2], tallies[2:2 + 2 * couples:2]
    room = jnp.minimum(source_of - 1, reach - receiver)
    moved = jax.random.randint(jax.random.fold_in(own_key, 1), (couples,), 0, 1 << 20) % (room + 1)
    tallies = tallies.at[1:1 + 2 * couples:2].set(source_of - moved).at[2:2 + 2 * couples:2].set(receiver + moved)
    return tallies[jax.random.permutation(jax.random.fold_in(own_key, 2), amount)]


def noise(stream_key, dims, width, reach, cuts=(), kind=jnp.bfloat16):
    values = jax.random.normal(stream_key, dims, jnp.float32) * width
    if len(cuts) > 0:
        values = shard_levels(stream_key, dims, cuts, -0.22, 0.18) * values
    return jnp.clip(values, min=-reach, max=reach).astype(kind)


def setup_inputs(seed: int = 0) -> dict:
    arg_keys = jax.random.split(jax.random.key(seed), 9)
    tokens = noise(arg_keys[0], (SAMPLES, N, D), 1.0, 6.0, ((1, 512),))
    chain_id = jnp.searchsorted(jnp.cumsum(ragged_sizes(arg_keys[1], CHAINS, N, N // 2, 0)), jnp.arange(N), side="right").astype(jnp.int32)
    hotspots = touch_ends(jax.random.randint(arg_keys[2], (HOT,), 0, N), jax.random.fold_in(arg_keys[2], 1), 0, N - 1).astype(jnp.int32)
    chain_embed = noise(arg_keys[3], (CHAINS, D), 1.0, 6.0)
    hot_embed = noise(arg_keys[4], (D,), 1.0, 6.0)
    w_proj = noise(arg_keys[5], (D, 4 * D), D ** -0.5, 0.21875, ((1, 16),))
    pair_bias = draw_pair_bias(jax.random.fold_in(arg_keys[8], 71), 0)
    w_out = noise(arg_keys[7], (D, D), D ** -0.5, 0.21875, ((0, 16),))
    return {"tokens": tokens, "chain_id": chain_id, "hotspots": hotspots, "chain_embed": chain_embed, "hot_embed": hot_embed, "w_proj": w_proj, "pair_bias": pair_bias, "w_out": w_out}


def attend_head(inputs):
    queries, keys, values, gating, bias_head = inputs
    block_rows = 512 if N % 512 == 0 else N
    blocks = N // block_rows
    query_blocks = jnp.moveaxis(queries.reshape(SAMPLES, blocks, block_rows, HD), 1, 0)
    gate_blocks = jnp.moveaxis(gating.reshape(SAMPLES, blocks, block_rows, HD), 1, 0)
    bias_blocks = bias_head.reshape(blocks, block_rows, N)

    def attend_rows(parts):
        query_rows, bias_rows, gate_rows = parts
        scores = jnp.einsum('sqd,skd->sqk', query_rows.astype(jnp.float32), keys.astype(jnp.float32))
        scores = scores + bias_rows.astype(jnp.float32)[None]
        row_max = lax.optimization_barrier(jnp.max(scores, axis=-1, keepdims=True))
        probs = jnp.exp(scores - row_max)
        row_sum = lax.optimization_barrier(jnp.sum(probs, axis=-1))
        rounded = probs.astype(jnp.bfloat16).astype(jnp.float32)
        weighted = jnp.einsum('sqk,skd->sqd', rounded, values.astype(jnp.float32))
        return (weighted / row_sum[..., None] * gate_rows).astype(jnp.bfloat16)
    result = lax.map(attend_rows, (query_blocks, bias_blocks, gate_blocks))
    return jnp.moveaxis(result, 0, 1).reshape(SAMPLES, N, HD)

def reference(tokens, chain_id, hotspots, chain_embed, hot_embed, w_proj, pair_bias, w_out):
    onehot = (chain_id[:, None] == jnp.arange(CHAINS, dtype=jnp.int32)[None, :]).astype(jnp.float32)
    is_hot = jnp.any(jnp.arange(N, dtype=jnp.int32)[:, None] == hotspots[None, :], axis=1).astype(jnp.float32)
    condition = lax.optimization_barrier(jnp.sum(onehot[:, :, None] * chain_embed.astype(jnp.float32)[None], axis=1))
    condition = condition + is_hot[:, None] * hot_embed.astype(jnp.float32)[None, :]
    shifted = tokens.astype(jnp.float32) + condition[None]
    average = lax.optimization_barrier(jnp.mean(shifted, axis=-1, keepdims=True))
    spread = lax.optimization_barrier(jnp.mean((shifted - average) ** 2, axis=-1, keepdims=True))
    normed = ((shifted - average) * lax.rsqrt(spread + 1e-05)).astype(jnp.bfloat16)
    proj = jnp.dot(normed.reshape(SAMPLES * N, D), w_proj, preferred_element_type=jnp.float32)
    proj = proj.reshape(SAMPLES, N, H, 4, HD)
    queries = (proj[:, :, :, 0] * (1.0 / HD ** 0.5)).astype(jnp.bfloat16)
    keys = proj[:, :, :, 1].astype(jnp.bfloat16)
    values = proj[:, :, :, 2].astype(jnp.bfloat16)
    gating = jax.nn.sigmoid(proj[:, :, :, 3])
    per_head = lax.map(attend_head, (jnp.moveaxis(queries, 2, 0), jnp.moveaxis(keys, 2, 0), jnp.moveaxis(values, 2, 0), jnp.moveaxis(gating, 2, 0), pair_bias))
    gated = jnp.moveaxis(per_head, 0, 2).reshape(SAMPLES * N, D)
    update = jnp.dot(gated, w_out, preferred_element_type=jnp.float32)
    return update.astype(jnp.bfloat16).reshape(SAMPLES, N, D)
```

```python
import functools

import jax
import jax.numpy as jnp
import numpy as np
from jax import lax
from jax.experimental import pallas as pl
from jax.experimental.pallas import tpu as pltpu
from jax.sharding import Mesh
from jax.sharding import PartitionSpec as P

HD = 48
AXES = ("y", "xlo", "core", "z", "xhi")
SIZES = (8, 2, 2, 8, 2)
HEADS = ("z", "xhi")
QUAD = ("xlo", "core")
F32, BF16 = jnp.float32, jnp.bfloat16
VMEM = 56 * 1024 * 1024


def params():
    return pltpu.CompilerParams(vmem_limit_bytes=VMEM)


def norm_kernel(first_ref, chain_ref, hot_ref, tok_ref, emb_ref, hemb_ref, out_ref):
    samples, tok_dev, width = tok_ref.shape
    first = first_ref[0]
    emb = emb_ref[...].astype(F32)
    hemb = hemb_ref[...].astype(F32)
    row_of = lax.broadcasted_iota(jnp.int32, (tok_dev, width), 0)
    cond = jnp.zeros((tok_dev, width), F32)
    for t in range(tok_dev):
        chain = chain_ref[t]
        row = jnp.zeros((1, width), F32)
        for c in range(emb_ref.shape[0]):
            row = row + jnp.where(chain == c, 1.0, 0.0) * emb[c : c + 1]
        hits = jnp.int32(0)
        for i in range(hot_ref.shape[0]):
            hits = hits + jnp.where(hot_ref[i] == first + t, 1, 0)
        row = row + jnp.where(hits > 0, 1.0, 0.0) * hemb
        cond = cond + jnp.where(row_of == t, row, 0.0)
    shifted = tok_ref[...].astype(F32) + cond[None]
    average = jnp.mean(shifted, axis=-1, keepdims=True)
    centred = shifted - average
    spread = jnp.mean(centred * centred, axis=-1, keepdims=True)
    normed = (centred * lax.rsqrt(spread + 1e-05)).reshape(samples * tok_dev, width).astype(BF16)
    for g in range(out_ref.shape[0]):
        out_ref[g] = normed


def proj_kernel(x_ref, wt_ref, q_ref, kv_ref, gate_ref):
    peers, rows, width = x_ref.shape
    samples = q_ref.shape[0]
    tok = rows // samples
    full = lax.dot_general(
        x_ref[...].reshape(peers * rows, width), wt_ref[...], (((1,), (1,)), ((), ())), preferred_element_type=F32
    ).reshape(peers, samples, tok, 4 * HD)
    for s in range(samples):
        one = full[:, s].reshape(peers * tok, 4 * HD)
        turned = jnp.transpose(one)
        q_ref[s] = (turned[:HD] * (1.0 / HD**0.5)).astype(BF16)
        kv_ref[s] = turned[HD : 3 * HD].astype(BF16)
        gate_ref[s] = jax.nn.sigmoid(turned[3 * HD :])


def attend_kernel(role_ref, q_ref, b0_ref, b1_ref, *refs):
    kv_refs, out_ref = refs[:-1], refs[-1]
    me, yy = role_ref[0], role_ref[1]
    keys = jnp.concatenate([r[0, :HD] for r in kv_refs], axis=1)
    vals = jnp.concatenate([r[0, HD:] for r in kv_refs], axis=1)
    shifts = (0, -1, 1, -2, 2, -3, 3, -4)
    lane = lax.broadcasted_iota(jnp.int32, (128, 128), 1)
    for role in range(4):
        src = b0_ref if role < 2 else b1_ref
        j = jnp.bitwise_xor(me, role)
        queries = jnp.transpose(q_ref[j, 0].astype(F32)).astype(BF16)
        scores = jnp.dot(queries, keys, preferred_element_type=F32)
        bias = [src[role % 2, lax.rem(yy + 8 + sh, 8)].astype(F32) for sh in shifts]
        scores = scores + jnp.concatenate(bias, axis=1)
        top = jnp.max(scores, axis=1, keepdims=True)
        probs = jnp.exp(scores - top)
        total = jnp.sum(probs, axis=1, keepdims=True)
        part = lax.dot_general(probs.astype(BF16), vals, (((1,), (1,)), ((), ())), preferred_element_type=F32)
        part = part / total
        lse = top + jnp.log(total)
        hi = lse.astype(BF16).astype(F32)
        mid = (lse - hi).astype(BF16).astype(F32)
        low = lse - hi - mid
        wide = jnp.concatenate([part, jnp.zeros((128, 128 - HD), F32)], axis=1)
        wide = jnp.where(lane == HD, hi, jnp.where(lane == HD + 1, mid, jnp.where(lane == HD + 2, low, wide)))
        out_ref[j, 0] = jnp.transpose(wide)[:64].astype(BF16)


def merge_kernel(p_ref, gate_ref, out_ref, wide_ref):
    parts, samples = p_ref.shape[:2]
    peers = out_ref.shape[0]
    for s in range(samples):
        rows = [p_ref[i, s].astype(F32) for i in range(parts)]
        lse = [r[HD : HD + 1] + r[HD + 1 : HD + 2] + r[HD + 2 : HD + 3] for r in rows]
        top = functools.reduce(jnp.maximum, lse)
        weight = [jnp.exp(v - top) for v in lse]
        mixed = sum(w * r[:HD] for w, r in zip(weight, rows)) / sum(weight) * gate_ref[s]
        wide = jnp.concatenate([mixed, jnp.zeros((128 - HD, 128), F32)], axis=0)
        turned = jnp.transpose(wide)
        tok = turned.shape[0] // peers
        wide_ref[:, s * tok : (s + 1) * tok] = turned.reshape(peers, tok, 128)
    out_ref[...] = wide_ref[:, :, :HD].astype(BF16)


def out_kernel(g_ref, w_ref, out_ref):
    heads = g_ref.shape[0]
    total = jnp.zeros(out_ref.shape, F32)
    for h in range(heads):
        total = total + jnp.dot(g_ref[h], w_ref[h], preferred_element_type=F32)
    out_ref[...] = total.astype(BF16)


def shift(x, axis, by):
    n = SIZES[AXES.index(axis)]
    return lax.ppermute(x, axis, [(i, (i + by) % n) for i in range(n)])


def half(x, dim, index):
    return lax.dynamic_index_in_dim(x, index, dim, keepdims=False)


def body(tokens, chain_id, hotspots, chain_embed, hot_embed, w_proj, pair_bias, w_out):
    samples, tok_dev, width = tokens.shape
    peers = lax.axis_size(HEADS)
    block = peers * tok_dev
    xlo, core, yy = lax.axis_index("xlo"), lax.axis_index("core"), lax.axis_index("y")
    first = (lax.axis_index(("y", "xlo", "core")) * peers + lax.axis_index(HEADS)) * tok_dev
    vm = pl.BlockSpec(memory_space=pltpu.VMEM)
    sm = pl.BlockSpec(memory_space=pltpu.SMEM)

    bias = pair_bias.reshape(block, 8, 2, 2, block)
    keep = jnp.transpose(half(bias, 3, core), (2, 1, 0, 3))
    away = jnp.transpose(half(bias, 3, 1 - core), (2, 1, 0, 3))
    pair = jnp.stack([keep, shift(away, "core", 1)], axis=1)
    bias0 = half(pair, 0, xlo)
    bias1 = shift(half(pair, 0, 1 - xlo), "xlo", 1)

    copies = pl.pallas_call(
        norm_kernel,
        out_shape=jax.ShapeDtypeStruct((peers, samples * tok_dev, width), BF16),
        in_specs=[sm, sm, sm, vm, vm, vm],
        out_specs=vm,
        compiler_params=params(),
    )(first[None], chain_id, hotspots, tokens, chain_embed, hot_embed[None])
    gathered = lax.all_to_all(copies, HEADS, split_axis=0, concat_axis=0, tiled=True)
    q_t, kv_t, gate_t = pl.pallas_call(
        proj_kernel,
        out_shape=(
            jax.ShapeDtypeStruct((samples, HD, block), BF16),
            jax.ShapeDtypeStruct((samples, 2 * HD, block), BF16),
            jax.ShapeDtypeStruct((samples, HD, block), F32),
        ),
        in_specs=[vm, vm],
        out_specs=(vm, vm, vm),
        compiler_params=params(),
    )(gathered, jnp.transpose(w_proj))

    w_mine, kv_t = lax.optimization_barrier((w_out, kv_t))
    w_full = lax.all_gather(w_mine, HEADS, axis=0)

    right, left, ring = kv_t, kv_t, [kv_t]
    for step in range(4):
        right = shift(right, "y", 1)
        ring.append(right)
        if step < 3:
            left = shift(left, "y", -1)
            ring.append(left)
    q_all = lax.all_gather(q_t, QUAD, axis=0)

    def per_sample(dims):
        return pl.BlockSpec((1,) + dims, lambda s, role: (s,) + (0,) * len(dims))

    def quad(dims):
        return pl.BlockSpec((4, 1) + dims, lambda s, role: (0, s) + (0,) * len(dims))

    whole = pl.BlockSpec((2, 8, block, block), lambda s, role: (0, 0, 0, 0))
    parts = pl.pallas_call(
        attend_kernel,
        out_shape=jax.ShapeDtypeStruct((4, samples, 64, block), BF16),
        grid_spec=pltpu.PrefetchScalarGridSpec(
            num_scalar_prefetch=1,
            grid=(samples,),
            in_specs=[quad((HD, block)), whole, whole] + [per_sample((2 * HD, block))] * 8,
            out_specs=quad((64, block)),
        ),
        compiler_params=params(),
    )(jnp.stack([xlo * 2 + core, yy]), q_all, bias0, bias1, *ring)
    mine = lax.all_to_all(parts, QUAD, split_axis=0, concat_axis=0, tiled=True)
    gated = pl.pallas_call(
        merge_kernel,
        out_shape=jax.ShapeDtypeStruct((peers, samples * tok_dev, HD), BF16),
        in_specs=[vm, vm],
        out_specs=vm,
        scratch_shapes=[pltpu.VMEM((peers, samples * tok_dev, 128), F32)],
        compiler_params=params(),
    )(mine, gate_t)
    heads = lax.all_to_all(gated, HEADS, split_axis=0, concat_axis=0, tiled=True)
    update = pl.pallas_call(
        out_kernel,
        out_shape=jax.ShapeDtypeStruct((samples * tok_dev, width), BF16),
        in_specs=[vm, vm],
        out_specs=vm,
        compiler_params=params(),
    )(heads, w_full)
    return update.reshape(samples, tok_dev, width)


def solution(mesh):
    fine = Mesh(np.asarray(mesh.devices).reshape(SIZES), AXES)
    blk = ("y", "xlo", "core")
    in_specs = (
        P(None, AXES, None),
        P(AXES),
        P(),
        P(),
        P(),
        P(None, HEADS),
        P(HEADS, blk, None),
        P(HEADS, None),
    )
    return jax.shard_map(body, mesh=fine, in_specs=in_specs, out_specs=P(None, AXES, None), check_vma=False)
```

```python
import functools

import jax
import jax.numpy as jnp
import numpy as np
from jax import lax
from jax.experimental import pallas as pl
from jax.experimental.pallas import tpu as pltpu
from jax.sharding import Mesh
from jax.sharding import PartitionSpec as P

HD = 48
AXES = ("y", "xlo", "core", "z", "xhi")
SIZES = (8, 2, 2, 8, 2)
HEADS = ("z", "xhi")
OCT = ("xlo", "core", "xhi")
F32, BF16 = jnp.float32, jnp.bfloat16
VMEM = 56 * 1024 * 1024
SHIFTS = (0, -1, 1, -2, 2, -3, 3, -4)


def params():
    return pltpu.CompilerParams(vmem_limit_bytes=VMEM)


def dot(a, b, da, db):
    return lax.dot_general(a, b, (((da,), (db,)), ((), ())), preferred_element_type=F32)


def norm_kernel(pos_ref, chain_ref, hot_ref, tok_ref, emb_ref, hemb_ref, out_ref):
    samples, tok_dev, width = tok_ref.shape
    first = pos_ref[0]
    emb = emb_ref[...].astype(F32)
    hemb = hemb_ref[...].astype(F32)
    row_of = lax.broadcasted_iota(jnp.int32, (tok_dev, width), 0)
    cond = jnp.zeros((tok_dev, width), F32)
    for t in range(tok_dev):
        chain = chain_ref[t]
        row = jnp.zeros((1, width), F32)
        for c in range(emb_ref.shape[0]):
            row = row + jnp.where(chain == c, 1.0, 0.0) * emb[c : c + 1]
        hits = jnp.int32(0)
        for i in range(hot_ref.shape[0]):
            hits = hits + jnp.where(hot_ref[i] == first + t, 1, 0)
        row = row + jnp.where(hits > 0, 1.0, 0.0) * hemb
        cond = cond + jnp.where(row_of == t, row, 0.0)
    shifted = tok_ref[...].astype(F32) + cond[None]
    average = jnp.mean(shifted, axis=-1, keepdims=True)
    centred = shifted - average
    spread = jnp.mean(centred * centred, axis=-1, keepdims=True)
    normed = (centred * lax.rsqrt(spread + 1e-05)).reshape(samples * tok_dev, width).astype(BF16)
    for g in range(out_ref.shape[0]):
        out_ref[g] = normed


def bias_kernel(pos_ref, b_ref, keep_ref, away_ref):
    xlo, core, xhi = pos_ref[1], pos_ref[2], pos_ref[3]
    row = lax.broadcasted_iota(jnp.int32, (128, 128), 0)
    col = lax.broadcasted_iota(jnp.int32, (128, 128), 1)
    z, t = (row % 64) // 8, row % 8
    from_q = (z * 2 + row // 64) * 8 + t
    from_k = (z * 2 + jnp.bitwise_xor(row // 64, xhi)) * 8 + t
    pick_q = jnp.where(col == from_q, 1.0, 0.0).astype(BF16)
    pick_k = jnp.where(col == from_k, 1.0, 0.0).astype(BF16)
    for b in range(32):
        y, xl, c = b // 4, (b // 2) % 2, b % 2
        tile = dot(pick_q, b_ref[0, :, b * 128 : (b + 1) * 128], 1, 0).astype(BF16)
        turned = dot(pick_k, tile, 1, 1).astype(BF16)
        role = jnp.bitwise_xor(xlo, xl)

        @pl.when(core == c)
        def _():
            keep_ref[role, y] = turned

        @pl.when(core != c)
        def _():
            away_ref[role, y] = turned


def proj_kernel(pos_ref, x_ref, own_ref, other_ref, q_ref, kv_own_ref, kv_other_ref, gate_ref):
    peers, rows, width = x_ref.shape
    pairs = kv_own_ref.shape[0]
    tok = rows // (2 * pairs)
    xhi = pos_ref[3]
    x = x_ref[...].reshape(peers * rows, width)
    for role, w_ref in enumerate((own_ref, other_ref)):
        kv_ref = (kv_own_ref, kv_other_ref)[role]
        full = dot(x, w_ref[: 4 * HD], 1, 1).reshape(peers, 2 * pairs, tok, 4 * HD)
        for p in range(pairs):
            two = jnp.concatenate([full[:, 2 * p + i].reshape(peers * tok, 4 * HD) for i in range(2)], axis=0)
            turned = jnp.transpose(two)
            queries = (turned[:HD] * (1.0 / HD**0.5)).astype(BF16)
            for d in range(4):
                q_ref[2 * d + jnp.bitwise_xor(xhi, role), p] = queries
            kv_ref[p] = turned[HD : 3 * HD].astype(BF16)
            gate_ref[jnp.bitwise_xor(xhi, role), p] = jax.nn.sigmoid(turned[3 * HD :])


def join(a, b):
    lane = lax.broadcasted_iota(jnp.int32, a.shape, 1)
    return jnp.where(lane < 64, a, pltpu.roll(b, 64, 1)), jnp.where(lane < 64, pltpu.roll(a, 64, 1), b)


def join_kernel(own_ref, other_ref, kv_ref):
    for p in range(own_ref.shape[0]):
        even, odd = join(own_ref[p].astype(F32), other_ref[p].astype(F32))
        kv_ref[2 * p] = even.astype(BF16)
        kv_ref[2 * p + 1] = odd.astype(BF16)


def join_q_kernel(pos_ref, q_ref, out_ref):
    me = pos_ref[1] * 2 + pos_ref[2]
    for role in range(4):
        d = 2 * jnp.bitwise_xor(me, role)
        for p in range(q_ref.shape[1]):
            even, odd = join(q_ref[d, p].astype(F32), q_ref[d + 1, p].astype(F32))
            out_ref[2 * p, :, role * 128 : (role + 1) * 128] = even.astype(BF16)
            out_ref[2 * p + 1, :, role * 128 : (role + 1) * 128] = odd.astype(BF16)


def attend_kernel(steps, first, last, pos_ref, q_ref, keep_ref, recv_ref, far_ref, *refs):
    count = sum(len(s) for s in steps)
    kv_refs, rest = refs[:count], refs[count:]
    me, yy = pos_ref[1] * 2 + pos_ref[2], pos_ref[0]
    acc = [None, None] if first else [rest[0][i] for i in range(2)]
    top = [None, None] if first else [rest[1][i, :1] for i in range(2)]
    at = 0
    for step in steps:
        bias = []
        for sh in step:
            y = lax.rem(yy + 8 + sh, 8)
            bias.append(
                jnp.concatenate([keep_ref[0, y], recv_ref[0, y], far_ref[0, y], far_ref[1, y]], axis=1).astype(F32)
            )
        bias = jnp.concatenate(bias, axis=0)
        blocks = kv_refs[at : at + len(step)]
        at += len(step)
        for i in range(2):
            keys = jnp.concatenate([jnp.transpose(r[i, :HD].astype(F32)).astype(BF16) for r in blocks], axis=0)
            vals = jnp.concatenate([r[i, HD:] for r in blocks], axis=1)
            vals = jnp.concatenate([vals, jnp.ones((16, vals.shape[1]), BF16)], axis=0)
            scores = jnp.dot(keys, q_ref[i], preferred_element_type=F32) + bias
            best = jnp.max(scores, axis=0, keepdims=True)
            if top[i] is not None:
                best = jnp.maximum(best, top[i])
            probs = jnp.exp(scores - best).astype(BF16)
            part = jnp.dot(vals, probs, preferred_element_type=F32)
            if top[i] is not None:
                part = part + acc[i] * jnp.exp(top[i] - best)
            acc[i], top[i] = part, best
    if not last:
        for i in range(2):
            rest[-2][i] = acc[i]
            rest[-1][i] = jnp.broadcast_to(top[i], (8, top[i].shape[1]))
        return
    out_ref = rest[-1]
    row = lax.broadcasted_iota(jnp.int32, (16, 128), 0)
    for role in range(4):
        d = 2 * jnp.bitwise_xor(me, role)
        tiles = []
        for i in range(2):
            mine = acc[i][:, role * 128 : (role + 1) * 128]
            total = mine[HD : HD + 1]
            lse = top[i][:, role * 128 : (role + 1) * 128] + jnp.log(total)
            hi = lse.astype(BF16).astype(F32)
            mid = (lse - hi).astype(BF16).astype(F32)
            low = lse - hi - mid
            tail = jnp.where(row == 0, hi, jnp.where(row == 1, mid, jnp.where(row == 2, low, 0.0)))
            tiles.append(jnp.concatenate([mine[:HD] / total, tail], axis=0))
        even, odd = join(tiles[0], tiles[1])
        out_ref[d, 0] = even.astype(BF16)
        out_ref[d + 1, 0] = odd.astype(BF16)


def merge_kernel(pos_ref, p_ref, gate_ref, w_own_ref, w_other_ref, out_ref):
    xhi = pos_ref[3]
    pairs = p_ref.shape[1]
    peers = out_ref.shape[0]
    for p in range(pairs):
        share = None
        for role, w_ref in enumerate((w_own_ref, w_other_ref)):
            h = jnp.bitwise_xor(xhi, role)
            rows = [p_ref[2 * i + h, p].astype(F32) for i in range(4)]
            lse = [r[HD : HD + 1] + r[HD + 1 : HD + 2] + r[HD + 2 : HD + 3] for r in rows]
            top = functools.reduce(jnp.maximum, lse)
            weight = [jnp.exp(v - top) for v in lse]
            mixed = sum(w * r[:HD] for w, r in zip(weight, rows)) / sum(weight) * gate_ref[h, p]
            gated = jnp.transpose(jnp.concatenate([mixed, jnp.zeros((80, 128), F32)], axis=0))[:, :HD].astype(BF16)
            term = jnp.dot(gated, w_ref[4 * HD :], preferred_element_type=F32)
            share = term if share is None else share + term
        tok = 64 // peers
        split = share.reshape(2, peers, tok, share.shape[1])
        for g in range(peers):
            both = jnp.concatenate([split[0, g], split[1, g]], axis=0)
            out_ref[g, 2 * tok * p : 2 * tok * (p + 1)] = both.astype(BF16)


def sum_kernel(x_ref, out_ref):
    total = x_ref[0].astype(F32)
    for g in range(1, x_ref.shape[0]):
        total = total + x_ref[g].astype(F32)
    out_ref[...] = total.astype(BF16)


def shift(x, axis, by):
    n = SIZES[AXES.index(axis)]
    return lax.ppermute(x, axis, [(i, (i + by) % n) for i in range(n)])


def body(tokens, chain_id, hotspots, chain_embed, hot_embed, w_proj, pair_bias, w_out):
    samples, tok_dev, width = tokens.shape
    pairs, peers = samples // 2, 8
    at = {a: lax.axis_index(a) for a in AXES}
    first = ((((at["y"] * 2 + at["xlo"]) * 2 + at["core"]) * 8 + at["z"]) * 2 + at["xhi"]) * tok_dev
    pos = jnp.stack([first, at["xlo"], at["core"], at["xhi"]])
    where = jnp.stack([at["y"], at["xlo"], at["core"], at["xhi"]])
    vm = pl.BlockSpec(memory_space=pltpu.VMEM)
    sm = pl.BlockSpec(memory_space=pltpu.SMEM)

    def call(kernel, specs, out, *args):
        shapes = [jax.ShapeDtypeStruct(s, t) for s, t in out]
        return pl.pallas_call(
            kernel, out_shape=shapes, in_specs=specs, out_specs=[vm] * len(out), compiler_params=params()
        )(*args)

    weights = jnp.concatenate([jnp.transpose(w_proj), w_out], axis=0)
    weights_other = shift(weights, "xhi", 1)
    keep, away = call(bias_kernel, [sm, vm], [((2, 8, 128, 128), BF16)] * 2, pos, pair_bias)
    recv = shift(away, "core", 1)
    far = shift(jnp.stack([keep[1], recv[1]]), "xlo", 1)

    (copies,) = call(
        norm_kernel,
        [sm, sm, sm, vm, vm, vm],
        [((peers, samples * tok_dev, width), BF16)],
        pos,
        chain_id,
        hotspots,
        tokens,
        chain_embed,
        hot_embed[None],
    )
    gathered = lax.all_to_all(copies, "z", split_axis=0, concat_axis=0, tiled=True)
    q_out, kv_own, kv_other, gate = call(
        proj_kernel,
        [sm, vm, vm, vm],
        [
            ((8, pairs, HD, 128), BF16),
            ((pairs, 2 * HD, 128), BF16),
            ((pairs, 2 * HD, 128), BF16),
            ((2, pairs, HD, 128), F32),
        ],
        pos,
        gathered,
        weights,
        weights_other,
    )
    kv_other = shift(kv_other, "xhi", 1)
    (kv,) = call(join_kernel, [vm, vm], [((samples, 2 * HD, 128), BF16)], kv_own, kv_other)
    right, left, ring = kv, kv, [kv]
    for step in range(4):
        right = shift(right, "y", 1)
        ring.append(right)
        if step < 3:
            left = shift(left, "y", -1)
            ring.append(left)
    q_in = lax.all_to_all(q_out, OCT, split_axis=0, concat_axis=0, tiled=True)
    (q_all,) = call(join_q_kernel, [sm, vm], [((samples, HD, 512), BF16)], pos, q_in)

    def two(*dims):
        return pl.BlockSpec((2,) + dims, lambda s, _: (s,) + (0,) * len(dims))

    whole = pl.BlockSpec((2, 8, 128, 128), lambda s, _: (0, 0, 0, 0))
    steps = (SHIFTS[0:2], SHIFTS[2:4], SHIFTS[4:6], SHIFTS[6:8])
    parts = pl.pallas_call(
        functools.partial(attend_kernel, steps, True, True),
        out_shape=jax.ShapeDtypeStruct((8, pairs, 64, 128), BF16),
        grid_spec=pltpu.PrefetchScalarGridSpec(
            num_scalar_prefetch=1,
            grid=(pairs,),
            in_specs=[two(HD, 512), whole, whole, whole] + [two(2 * HD, 128)] * 8,
            out_specs=pl.BlockSpec((8, 1, 64, 128), lambda s, _: (0, s, 0, 0)),
        ),
        compiler_params=params(),
    )(where, q_all, keep, recv, far, *ring)
    mine = lax.all_to_all(parts, OCT, split_axis=0, concat_axis=0, tiled=True)
    (shares,) = call(
        merge_kernel,
        [sm, vm, vm, vm, vm],
        [((peers, samples * tok_dev, width), BF16)],
        pos,
        mine,
        gate,
        weights,
        weights_other,
    )
    summands = lax.all_to_all(shares, "z", split_axis=0, concat_axis=0, tiled=True)
    (update,) = call(sum_kernel, [vm], [((samples * tok_dev, width), BF16)], summands)
    return update.reshape(samples, tok_dev, width)


def solution(mesh):
    fine = Mesh(np.asarray(mesh.devices).reshape(SIZES), AXES)
    blk = ("y", "xlo", "core")
    in_specs = (
        P(None, AXES, None),
        P(AXES),
        P(),
        P(),
        P(),
        P(None, HEADS),
        P(HEADS, blk, None),
        P(HEADS, None),
    )
    return jax.shard_map(body, mesh=fine, in_specs=in_specs, out_specs=P(None, AXES, None), check_vma=False)
```

```python
import functools

import jax
import jax.numpy as jnp
import numpy as np
from jax import lax
from jax.experimental import pallas as pl
from jax.experimental.pallas import tpu as pltpu
from jax.sharding import Mesh
from jax.sharding import PartitionSpec as P

HD = 48
AXES = ("y", "xlo", "core", "z", "xhi")
SIZES = (8, 2, 2, 8, 2)
HEADS = ("z", "xhi")
OCT = ("xlo", "core", "xhi")
F32, BF16 = jnp.float32, jnp.bfloat16
VMEM = 56 * 1024 * 1024


def params():
    return pltpu.CompilerParams(vmem_limit_bytes=VMEM)


def dot(a, b, da, db):
    return lax.dot_general(a, b, (((da,), (db,)), ((), ())), preferred_element_type=F32)


def norm_kernel(pos_ref, chain_ref, hot_ref, tok_ref, emb_ref, hemb_ref, out_ref):
    samples, tok_dev, width = tok_ref.shape
    first = pos_ref[0]
    emb = emb_ref[...].astype(F32)
    hemb = hemb_ref[...].astype(F32)
    row_of = lax.broadcasted_iota(jnp.int32, (tok_dev, width), 0)
    cond = jnp.zeros((tok_dev, width), F32)
    for t in range(tok_dev):
        chain = chain_ref[t]
        row = jnp.zeros((1, width), F32)
        for c in range(emb_ref.shape[0]):
            row = row + jnp.where(chain == c, 1.0, 0.0) * emb[c : c + 1]
        hits = jnp.int32(0)
        for i in range(hot_ref.shape[0]):
            hits = hits + jnp.where(hot_ref[i] == first + t, 1, 0)
        row = row + jnp.where(hits > 0, 1.0, 0.0) * hemb
        cond = cond + jnp.where(row_of == t, row, 0.0)
    shifted = tok_ref[...].astype(F32) + cond[None]
    average = jnp.mean(shifted, axis=-1, keepdims=True)
    centred = shifted - average
    spread = jnp.mean(centred * centred, axis=-1, keepdims=True)
    normed = (centred * lax.rsqrt(spread + 1e-05)).reshape(samples * tok_dev, width).astype(BF16)
    for g in range(out_ref.shape[0]):
        out_ref[g] = normed


def bias_kernel(pos_ref, b_ref, keep_ref, away_ref, rows_ref):
    xlo, core, xhi = pos_ref[1], pos_ref[2], pos_ref[3]
    row = lax.broadcasted_iota(jnp.int32, (128, 128), 0)
    col = lax.broadcasted_iota(jnp.int32, (128, 128), 1)
    z, t = (row % 64) // 8, row % 8
    from_q = (z * 2 + row // 64) * 8 + t
    from_k = (z * 2 + jnp.bitwise_xor(row // 64, xhi)) * 8 + t
    pick_q = jnp.where(col == from_q, 1.0, 0.0).astype(BF16)
    pick_k = jnp.where(col == from_k, 1.0, 0.0).astype(BF16)
    for b in range(32):
        rows_ref[b] = dot(pick_q, b_ref[0, :, b * 128 : (b + 1) * 128], 1, 0).astype(BF16)
    for role in range(2):
        xl = jnp.bitwise_xor(xlo, role)
        for y in range(8):
            at = (y * 2 + xl) * 2
            keep_ref[role, y] = dot(pick_k, rows_ref[at + core], 1, 1).astype(BF16)
            away_ref[role, y] = dot(pick_k, rows_ref[at + 1 - core], 1, 1).astype(BF16)


def proj_kernel(pos_ref, x_ref, own_ref, other_ref, q_ref, kv_own_ref, kv_other_ref, gate_ref):
    peers, rows, width = x_ref.shape
    pairs = kv_own_ref.shape[0]
    tok = rows // (2 * pairs)
    xhi = pos_ref[3]
    x = x_ref[...].reshape(peers * rows, width)
    for role, w_ref in enumerate((own_ref, other_ref)):
        kv_ref = (kv_own_ref, kv_other_ref)[role]
        full = dot(x, w_ref[: 4 * HD], 1, 1).reshape(peers, 2 * pairs, tok, 4 * HD)
        for p in range(pairs):
            two = jnp.concatenate([full[:, 2 * p + i].reshape(peers * tok, 4 * HD) for i in range(2)], axis=0)
            turned = jnp.transpose(two)
            queries = (turned[:HD] * (1.0 / HD**0.5)).astype(BF16)
            for d in range(4):
                q_ref[2 * d + jnp.bitwise_xor(xhi, role), p] = queries
            kv_ref[p] = turned[HD : 3 * HD].astype(BF16)
            gate_ref[jnp.bitwise_xor(xhi, role), p] = jax.nn.sigmoid(turned[3 * HD :])


def join(a, b):
    lane = lax.broadcasted_iota(jnp.int32, a.shape, 1)
    return jnp.where(lane < 64, a, pltpu.roll(b, 64, 1)), jnp.where(lane < 64, pltpu.roll(a, 64, 1), b)


def join_kernel(own_ref, other_ref, first_ref, second_ref):
    pairs = own_ref.shape[0]
    for p in range(pairs):
        half, at = divmod(p, pairs // 2)
        out_ref = (first_ref, second_ref)[half]
        both = join(own_ref[p].astype(F32), other_ref[p].astype(F32))
        for i in range(2):
            one = both[i].astype(BF16)
            for y in range(out_ref.shape[0]):
                out_ref[y, 2 * at + i] = one


def join_q_kernel(pos_ref, q_ref, out_ref):
    me = pos_ref[1] * 2 + pos_ref[2]
    for role in range(4):
        d = 2 * jnp.bitwise_xor(me, role)
        for p in range(q_ref.shape[1]):
            even, odd = join(q_ref[d, p].astype(F32), q_ref[d + 1, p].astype(F32))
            out_ref[2 * p, :, role * 128 : (role + 1) * 128] = even.astype(BF16)
            out_ref[2 * p + 1, :, role * 128 : (role + 1) * 128] = odd.astype(BF16)


def attend_kernel(pos_ref, q_ref, keep_ref, recv_ref, far_ref, kv_ref, out_ref):
    me = pos_ref[1] * 2 + pos_ref[2]
    acc, top = [None, None], [None, None]
    for y in range(0, 8, 2):
        bias = [
            jnp.concatenate([keep_ref[0, b], recv_ref[0, b], far_ref[0, b], far_ref[1, b]], axis=1).astype(F32)
            for b in (y, y + 1)
        ]
        bias = jnp.concatenate(bias, axis=0)
        for i in range(2):
            keys = [jnp.transpose(kv_ref[b, i, :HD].astype(F32)).astype(BF16) for b in (y, y + 1)]
            keys = jnp.concatenate(keys, axis=0)
            vals = jnp.concatenate([kv_ref[y, i, HD:], kv_ref[y + 1, i, HD:]], axis=1)
            vals = jnp.concatenate([vals, jnp.ones((16, vals.shape[1]), BF16)], axis=0)
            scores = jnp.dot(keys, q_ref[i], preferred_element_type=F32) + bias
            best = jnp.max(scores, axis=0, keepdims=True)
            if top[i] is not None:
                best = jnp.maximum(best, top[i])
            probs = jnp.exp(scores - best).astype(BF16)
            part = jnp.dot(vals, probs, preferred_element_type=F32)
            if top[i] is not None:
                part = part + acc[i] * jnp.exp(top[i] - best)
            acc[i], top[i] = part, best
    row = lax.broadcasted_iota(jnp.int32, (16, 128), 0)
    for role in range(4):
        d = 2 * jnp.bitwise_xor(me, role)
        tiles = []
        for i in range(2):
            mine = acc[i][:, role * 128 : (role + 1) * 128]
            total = mine[HD : HD + 1]
            lse = top[i][:, role * 128 : (role + 1) * 128] + jnp.log(total)
            hi = lse.astype(BF16).astype(F32)
            mid = (lse - hi).astype(BF16).astype(F32)
            low = lse - hi - mid
            tail = jnp.where(row == 0, hi, jnp.where(row == 1, mid, jnp.where(row == 2, low, 0.0)))
            tiles.append(jnp.concatenate([mine[:HD] / total, tail], axis=0))
        even, odd = join(tiles[0], tiles[1])
        out_ref[d, 0] = even.astype(BF16)
        out_ref[d + 1, 0] = odd.astype(BF16)


def merge_kernel(pos_ref, first_ref, second_ref, gate_ref, out_ref):
    xhi = pos_ref[3]
    per_half = first_ref.shape[1]
    peers = out_ref.shape[0]
    tok = 64 // peers
    for p in range(2 * per_half):
        half, at = divmod(p, per_half)
        p_ref = (first_ref, second_ref)[half]
        gated = []
        for role in range(2):
            h = jnp.bitwise_xor(xhi, role)
            rows = [p_ref[2 * i + h, at].astype(F32) for i in range(4)]
            lse = [r[HD : HD + 1] + r[HD + 1 : HD + 2] + r[HD + 2 : HD + 3] for r in rows]
            top = functools.reduce(jnp.maximum, lse)
            weight = [jnp.exp(v - top) for v in lse]
            gated.append(sum(w * r[:HD] for w, r in zip(weight, rows)) / sum(weight) * gate_ref[h, p])
        turned = jnp.transpose(jnp.concatenate(gated + [jnp.zeros((128 - 2 * HD, 128), F32)], axis=0))
        split = turned.reshape(2, peers, tok, 128)
        for g in range(peers):
            both = jnp.concatenate([split[0, g], split[1, g]], axis=0)
            out_ref[g, 2 * tok * p : 2 * tok * (p + 1)] = both.astype(BF16)


def out_kernel(pos_ref, g_ref, *refs):
    w_refs, out_ref = refs[:-1], refs[-1]
    total = None
    for by, w_ref in enumerate(w_refs):
        gated = g_ref[lax.rem(pos_ref[4] + 8 - by, 8)]
        term = jnp.dot(gated[:, : 2 * HD], w_ref[...], preferred_element_type=F32)
        total = term if total is None else total + term
    out_ref[...] = total.astype(BF16)


def shift(x, axis, by):
    n = SIZES[AXES.index(axis)]
    return lax.ppermute(x, axis, [(i, (i + by) % n) for i in range(n)])


def body(tokens, chain_id, hotspots, chain_embed, hot_embed, w_proj, pair_bias, w_out):
    samples, tok_dev, width = tokens.shape
    pairs, peers = samples // 2, 8
    at = {a: lax.axis_index(a) for a in AXES}
    first = ((((at["y"] * 2 + at["xlo"]) * 2 + at["core"]) * 8 + at["z"]) * 2 + at["xhi"]) * tok_dev
    pos = jnp.stack([first, at["xlo"], at["core"], at["xhi"], at["z"]])
    vm = pl.BlockSpec(memory_space=pltpu.VMEM)
    sm = pl.BlockSpec(memory_space=pltpu.SMEM)

    def call(kernel, specs, out, *args, scratch=()):
        shapes = [jax.ShapeDtypeStruct(s, t) for s, t in out]
        return pl.pallas_call(
            kernel,
            out_shape=shapes,
            in_specs=specs,
            out_specs=[vm] * len(out),
            scratch_shapes=scratch,
            compiler_params=params(),
        )(*args)

    def exchange(x, axes):
        return lax.all_to_all(x, axes, split_axis=0, concat_axis=0, tiled=True)

    weights = jnp.concatenate([jnp.transpose(w_proj), w_out], axis=0)
    weights_other = shift(weights, "xhi", 1)
    keep, away = call(
        bias_kernel,
        [sm, vm],
        [((2, 8, 128, 128), BF16)] * 2,
        pos,
        pair_bias,
        scratch=[pltpu.VMEM((32, 128, 128), BF16)],
    )
    recv = shift(away, "core", 1)
    far_out = jnp.stack([keep[1], recv[1]])

    (copies,) = call(
        norm_kernel,
        [sm, sm, sm, vm, vm, vm],
        [((peers, samples * tok_dev, width), BF16)],
        pos,
        chain_id,
        hotspots,
        tokens,
        chain_embed,
        hot_embed[None],
    )
    gathered, far_out = lax.optimization_barrier((exchange(copies, "z"), far_out))
    far = shift(far_out, "xlo", 1)
    q_out, kv_own, kv_other, gate = call(
        proj_kernel,
        [sm, vm, vm, vm],
        [
            ((8, pairs, HD, 128), BF16),
            ((pairs, 2 * HD, 128), BF16),
            ((pairs, 2 * HD, 128), BF16),
            ((2, pairs, HD, 128), F32),
        ],
        pos,
        gathered,
        weights,
        weights_other,
    )
    kv_other, q_in = lax.optimization_barrier((shift(kv_other, "xhi", 1), exchange(q_out, OCT)))
    half = samples // 2
    kv = call(join_kernel, [vm, vm], [((8, half, 2 * HD, 128), BF16)] * 2, kv_own, kv_other)
    w_rows = jnp.concatenate([weights[4 * HD :], weights_other[4 * HD :]], axis=0)
    w_rows, kv_first = lax.optimization_barrier((w_rows, kv[0]))
    w_all = [w_rows] + [shift(w_rows, "z", by) for by in range(1, peers)]
    (q_all,) = call(join_q_kernel, [sm, vm], [((samples, HD, 512), BF16)], pos, q_in)
    kv_first, kv_second, far, q_all, *w_all[1:5] = lax.optimization_barrier(
        (exchange(kv_first, "y"), kv[1], far, q_all, *w_all[1:5])
    )
    kv_second, *w_all[5:] = lax.optimization_barrier((exchange(kv_second, "y"), *w_all[5:]))
    kv_in = [kv_first, kv_second]

    whole = pl.BlockSpec((2, 8, 128, 128), lambda s, _: (0, 0, 0, 0))
    mine = []
    for part in range(2):
        steps = pairs // 2
        result = pl.pallas_call(
            attend_kernel,
            out_shape=jax.ShapeDtypeStruct((8, steps, 64, 128), BF16),
            grid_spec=pltpu.PrefetchScalarGridSpec(
                num_scalar_prefetch=1,
                grid=(steps,),
                in_specs=[
                    pl.BlockSpec((2, HD, 512), lambda s, _, base=part * steps: (base + s, 0, 0)),
                    whole,
                    whole,
                    whole,
                    pl.BlockSpec((8, 2, 2 * HD, 128), lambda s, _: (0, s, 0, 0)),
                ],
                out_specs=pl.BlockSpec((8, 1, 64, 128), lambda s, _: (0, s, 0, 0)),
            ),
            compiler_params=params(),
            cost_estimate=pl.CostEstimate(flops=4 * half * 512 * 1024 * 64, bytes_accessed=5 << 20, transcendentals=half << 19),
        )(pos, q_all, keep, recv, far, kv_in[part])
        if part == 0:
            result, kv_in[1] = lax.optimization_barrier((result, kv_in[1]))
        mine.append(exchange(result, OCT))
    (gated,) = call(
        merge_kernel,
        [sm, vm, vm, vm],
        [((peers, samples * tok_dev, 128), BF16)],
        pos,
        mine[0],
        mine[1],
        gate,
    )
    (update,) = call(
        out_kernel,
        [sm, vm] + [vm] * peers,
        [((samples * tok_dev, width), BF16)],
        pos,
        exchange(gated, "z"),
        *w_all,
    )
    return update.reshape(samples, tok_dev, width)


def solution(mesh):
    fine = Mesh(np.asarray(mesh.devices).reshape(SIZES), AXES)
    blk = ("y", "xlo", "core")
    in_specs = (
        P(None, AXES, None),
        P(AXES),
        P(),
        P(),
        P(),
        P(None, HEADS),
        P(HEADS, blk, None),
        P(HEADS, None),
    )
    return jax.shard_map(body, mesh=fine, in_specs=in_specs, out_specs=P(None, AXES, None), check_vma=False)
```

```python
import functools

import jax
import jax.numpy as jnp
import numpy as np
from jax import lax
from jax.experimental import pallas as pl
from jax.experimental.pallas import tpu as pltpu
from jax.sharding import Mesh
from jax.sharding import PartitionSpec as P

HD = 48
AXES = ("y", "xlo", "core", "z", "xhi")
SIZES = (8, 2, 2, 8, 2)
HEADS = ("z", "xhi")
OCT = ("xlo", "core", "xhi")
F32, BF16 = jnp.float32, jnp.bfloat16
VMEM = 56 * 1024 * 1024


def params():
    return pltpu.CompilerParams(vmem_limit_bytes=VMEM)


def dot(a, b, da, db):
    return lax.dot_general(a, b, (((da,), (db,)), ((), ())), preferred_element_type=F32)


def norm_kernel(pos_ref, chain_ref, hot_ref, tok_ref, emb_ref, hemb_ref, out_ref):
    samples, tok_dev, width = tok_ref.shape
    first = pos_ref[0]
    emb = emb_ref[...].astype(F32)
    hemb = hemb_ref[...].astype(F32).reshape(1, width)
    row_of = lax.broadcasted_iota(jnp.int32, (tok_dev, width), 0)
    cond = jnp.zeros((tok_dev, width), F32)
    for t in range(tok_dev):
        chain = chain_ref[t]
        row = jnp.zeros((1, width), F32)
        for c in range(emb_ref.shape[0]):
            row = row + jnp.where(chain == c, 1.0, 0.0) * emb[c : c + 1]
        hits = jnp.int32(0)
        for i in range(hot_ref.shape[0]):
            hits = hits + jnp.where(hot_ref[i] == first + t, 1, 0)
        row = row + jnp.where(hits > 0, 1.0, 0.0) * hemb
        cond = cond + jnp.where(row_of == t, row, 0.0)
    shifted = tok_ref[...].astype(F32) + cond[None]
    average = jnp.mean(shifted, axis=-1, keepdims=True)
    centred = shifted - average
    spread = jnp.mean(centred * centred, axis=-1, keepdims=True)
    normed = (centred * lax.rsqrt(spread + 1e-05)).reshape(samples * tok_dev, width).astype(BF16)
    for g in range(out_ref.shape[0]):
        out_ref[g] = normed


def bias_kernel(pos_ref, b_ref, keep_ref, away_ref, rows_ref):
    xlo, core, xhi = pos_ref[1], pos_ref[2], pos_ref[3]
    row = lax.broadcasted_iota(jnp.int32, (128, 128), 0)
    col = lax.broadcasted_iota(jnp.int32, (128, 128), 1)
    z, t = (row % 64) // 8, row % 8
    from_q = (z * 2 + row // 64) * 8 + t
    from_k = (z * 2 + jnp.bitwise_xor(row // 64, xhi)) * 8 + t
    pick_q = jnp.where(col == from_q, 1.0, 0.0).astype(BF16)
    pick_k = jnp.where(col == from_k, 1.0, 0.0).astype(BF16)
    for b in range(32):
        rows_ref[b] = dot(pick_q, b_ref[0, :, b * 128 : (b + 1) * 128], 1, 0).astype(BF16)
    for role in range(2):
        xl = jnp.bitwise_xor(xlo, role)
        for y in range(8):
            at = (y * 2 + xl) * 2
            keep_ref[role, y] = dot(pick_k, rows_ref[at + core], 1, 1).astype(BF16)
            away_ref[role, y] = dot(pick_k, rows_ref[at + 1 - core], 1, 1).astype(BF16)


def proj_kernel(pos_ref, x_ref, own_ref, other_ref, q_ref, kv_own_ref, kv_other_ref, gate_ref):
    peers, rows, width = x_ref.shape
    pairs = kv_own_ref.shape[0]
    tok = rows // (2 * pairs)
    xhi = pos_ref[3]
    x = x_ref[...].reshape(peers * rows, width)
    for role, w_ref in enumerate((own_ref, other_ref)):
        kv_ref = (kv_own_ref, kv_other_ref)[role]
        full = dot(x, w_ref[: 4 * HD], 1, 1).reshape(peers, 2 * pairs, tok, 4 * HD)
        for p in range(pairs):
            two = jnp.concatenate([full[:, 2 * p + i].reshape(peers * tok, 4 * HD) for i in range(2)], axis=0)
            turned = jnp.transpose(two)
            queries = (turned[:HD] * (1.0 / HD**0.5)).astype(BF16)
            for d in range(4):
                q_ref[2 * d + jnp.bitwise_xor(xhi, role), p] = queries
            kv_ref[p] = turned[HD : 3 * HD].astype(BF16)
            gate_ref[jnp.bitwise_xor(xhi, role), p] = jax.nn.sigmoid(turned[3 * HD :])


def join(a, b):
    lane = lax.broadcasted_iota(jnp.int32, a.shape, 1)
    return jnp.where(lane < 64, a, pltpu.roll(b, 64, 1)), jnp.where(lane < 64, pltpu.roll(a, 64, 1), b)


def join_kernel(own_ref, other_ref, kv_ref):
    for p in range(own_ref.shape[0]):
        even, odd = join(own_ref[p].astype(F32), other_ref[p].astype(F32))
        kv_ref[2 * p] = even.astype(BF16)
        kv_ref[2 * p + 1] = odd.astype(BF16)


def join_q_kernel(pos_ref, q_ref, out_ref):
    me = pos_ref[1] * 2 + pos_ref[2]
    for role in range(4):
        d = 2 * jnp.bitwise_xor(me, role)
        for p in range(q_ref.shape[1]):
            even, odd = join(q_ref[d, p].astype(F32), q_ref[d + 1, p].astype(F32))
            out_ref[2 * p, :, role * 128 : (role + 1) * 128] = even.astype(BF16)
            out_ref[2 * p + 1, :, role * 128 : (role + 1) * 128] = odd.astype(BF16)


def attend_kernel(steps, first, last, pos_ref, q_ref, keep_ref, recv_ref, far_ref, *refs):
    count = sum(len(s) for s in steps)
    kv_refs, rest = refs[:count], refs[count:]
    me, yy = pos_ref[1] * 2 + pos_ref[2], pos_ref[4]
    acc = [None, None] if first else [rest[0][i] for i in range(2)]
    top = [None, None] if first else [rest[1][i, :1] for i in range(2)]
    at = 0
    for step in steps:
        bias = []
        for sh in step:
            y = lax.rem(yy + 8 + sh, 8)
            bias.append(
                jnp.concatenate([keep_ref[0, y], recv_ref[0, y], far_ref[0, y], far_ref[1, y]], axis=1).astype(F32)
            )
        bias = jnp.concatenate(bias, axis=0)
        blocks = kv_refs[at : at + len(step)]
        at += len(step)
        for i in range(2):
            keys = jnp.concatenate([jnp.transpose(r[i, :HD].astype(F32)).astype(BF16) for r in blocks], axis=0)
            vals = jnp.concatenate([r[i, HD:] for r in blocks], axis=1)
            vals = jnp.concatenate([vals, jnp.ones((16, vals.shape[1]), BF16)], axis=0)
            scores = jnp.dot(keys, q_ref[i], preferred_element_type=F32) + bias
            best = jnp.max(scores, axis=0, keepdims=True)
            if top[i] is not None:
                best = jnp.maximum(best, top[i])
            probs = jnp.exp(scores - best).astype(BF16)
            part = jnp.dot(vals, probs, preferred_element_type=F32)
            if top[i] is not None:
                part = part + acc[i] * jnp.exp(top[i] - best)
            acc[i], top[i] = part, best
    if not last:
        for i in range(2):
            rest[-2][i] = acc[i]
            rest[-1][i] = jnp.broadcast_to(top[i], (8, top[i].shape[1]))
        return
    out_ref = rest[-1]
    row = lax.broadcasted_iota(jnp.int32, (16, 128), 0)
    for role in range(4):
        d = 2 * jnp.bitwise_xor(me, role)
        tiles = []
        for i in range(2):
            mine = acc[i][:, role * 128 : (role + 1) * 128]
            total = mine[HD : HD + 1]
            lse = top[i][:, role * 128 : (role + 1) * 128] + jnp.log(total)
            hi = lse.astype(BF16).astype(F32)
            mid = (lse - hi).astype(BF16).astype(F32)
            low = lse - hi - mid
            tail = jnp.where(row == 0, hi, jnp.where(row == 1, mid, jnp.where(row == 2, low, 0.0)))
            tiles.append(jnp.concatenate([mine[:HD] / total, tail], axis=0))
        even, odd = join(tiles[0], tiles[1])
        out_ref[d, 0] = even.astype(BF16)
        out_ref[d + 1, 0] = odd.astype(BF16)


def merge_kernel(pos_ref, p_ref, gate_ref, w_own_ref, w_other_ref, out_ref):
    xhi = pos_ref[3]
    pairs = p_ref.shape[1]
    peers = out_ref.shape[0]
    for p in range(pairs):
        share = None
        for role, w_ref in enumerate((w_own_ref, w_other_ref)):
            h = jnp.bitwise_xor(xhi, role)
            rows = [p_ref[2 * i + h, p].astype(F32) for i in range(4)]
            lse = [r[HD : HD + 1] + r[HD + 1 : HD + 2] + r[HD + 2 : HD + 3] for r in rows]
            top = functools.reduce(jnp.maximum, lse)
            weight = [jnp.exp(v - top) for v in lse]
            mixed = sum(w * r[:HD] for w, r in zip(weight, rows)) / sum(weight) * gate_ref[h, p]
            gated = jnp.transpose(jnp.concatenate([mixed, jnp.zeros((80, 128), F32)], axis=0))[:, :HD].astype(BF16)
            term = jnp.dot(gated, w_ref[4 * HD :], preferred_element_type=F32)
            share = term if share is None else share + term
        tok = 64 // peers
        split = share.reshape(2, peers, tok, share.shape[1])
        for g in range(peers):
            both = jnp.concatenate([split[0, g], split[1, g]], axis=0)
            out_ref[g, 2 * tok * p : 2 * tok * (p + 1)] = both.astype(BF16)


def sum_kernel(x_ref, out_ref):
    total = x_ref[0].astype(F32)
    for g in range(1, x_ref.shape[0]):
        total = total + x_ref[g].astype(F32)
    out_ref[...] = total.astype(BF16)


def shift(x, axis, by):
    n = SIZES[AXES.index(axis)]
    return lax.ppermute(x, axis, [(i, (i + by) % n) for i in range(n)])


def body(tokens, chain_id, hotspots, chain_embed, hot_embed, w_proj, pair_bias, w_out):
    samples, tok_dev, width = tokens.shape
    pairs, peers = samples // 2, 8
    at = {a: lax.axis_index(a) for a in AXES}
    first = ((((at["y"] * 2 + at["xlo"]) * 2 + at["core"]) * 8 + at["z"]) * 2 + at["xhi"]) * tok_dev
    pos = jnp.stack([first, at["xlo"], at["core"], at["xhi"], at["y"]])
    vm = pl.BlockSpec(memory_space=pltpu.VMEM)
    sm = pl.BlockSpec(memory_space=pltpu.SMEM)

    def call(kernel, specs, out, *args, scratch=()):
        shapes = [jax.ShapeDtypeStruct(s, t) for s, t in out]
        return pl.pallas_call(
            kernel,
            out_shape=shapes,
            in_specs=specs,
            out_specs=[vm] * len(out),
            scratch_shapes=scratch,
            compiler_params=params(),
        )(*args)

    def exchange(x, axes):
        return lax.all_to_all(x, axes, split_axis=0, concat_axis=0, tiled=True)

    weights = jnp.concatenate([jnp.transpose(w_proj), w_out], axis=0)
    weights_other = shift(weights, "xhi", 1)
    keep, away = call(
        bias_kernel,
        [sm, vm],
        [((2, 8, 128, 128), BF16)] * 2,
        pos,
        pair_bias,
        scratch=[pltpu.VMEM((32, 128, 128), BF16)],
    )
    recv = shift(away, "core", 1)
    far_out = jnp.stack([keep[1], recv[1]])

    (copies,) = call(
        norm_kernel,
        [sm, sm, sm, vm, vm, vm],
        [((peers, samples * tok_dev, width), BF16)],
        pos,
        chain_id,
        hotspots,
        tokens,
        chain_embed,
        hot_embed,
    )
    gathered = exchange(copies, "z")
    weights_other, far_out = lax.optimization_barrier((weights_other, far_out))
    far = shift(far_out, "xlo", 1)
    gathered, far_out = lax.optimization_barrier((gathered, far_out))
    q_out, kv_own, kv_other, gate = call(
        proj_kernel,
        [sm, vm, vm, vm],
        [
            ((8, pairs, HD, 128), BF16),
            ((pairs, 2 * HD, 128), BF16),
            ((pairs, 2 * HD, 128), BF16),
            ((2, pairs, HD, 128), F32),
        ],
        pos,
        gathered,
        weights,
        weights_other,
    )
    kv_other = shift(kv_other, "xhi", 1)
    (kv,) = call(join_kernel, [vm, vm], [((samples, 2 * HD, 128), BF16)], kv_own, kv_other)

    def two(*dims):
        return pl.BlockSpec((2,) + dims, lambda s, _: (s,) + (0,) * len(dims))

    whole = pl.BlockSpec((2, 8, 128, 128), lambda s, _: (0, 0, 0, 0))
    state_shape = (jax.ShapeDtypeStruct((samples, 64, 512), F32), jax.ShapeDtypeStruct((samples, 8, 512), F32))

    def attend(state, steps, blocks, last=False):
        carried = [] if state is None else list(state)
        out = jax.ShapeDtypeStruct((8, pairs, 64, 128), BF16) if last else state_shape
        out_specs = pl.BlockSpec((8, 1, 64, 128), lambda s, _: (0, s, 0, 0)) if last else (two(64, 512), two(8, 512))
        count = len(blocks)
        return pl.pallas_call(
            functools.partial(attend_kernel, steps, state is None, last),
            out_shape=out,
            grid_spec=pltpu.PrefetchScalarGridSpec(
                num_scalar_prefetch=1,
                grid=(pairs,),
                in_specs=[two(HD, 512), whole, whole, whole]
                + [two(2 * HD, 128)] * count
                + [two(64, 512), two(8, 512)][: len(carried)],
                out_specs=out_specs,
            ),
            compiler_params=params(),
            cost_estimate=pl.CostEstimate(
                flops=count * (1 << 30), bytes_accessed=3 << 20, transcendentals=count << 19
            ),
        )(pos, q_all, keep, recv, far, *blocks, *carried)

    def tie(x, dep):
        return lax.optimization_barrier((x, dep))

    kv, q_out, far = lax.optimization_barrier((kv, q_out, far))
    r1, l1 = shift(kv, "y", 1), shift(kv, "y", -1)
    q_in = exchange(q_out, OCT)
    (q_all,) = call(join_q_kernel, [sm, vm], [((samples, HD, 512), BF16)], pos, q_in)
    r2 = shift(r1, "y", 1)
    state = attend(None, ((0,),), [kv])
    l1, state = tie(l1, state)
    l2 = shift(l1, "y", -1)
    state = attend(state, ((-1,),), [r1])
    r2, state = tie(r2, state)
    r3 = shift(r2, "y", 1)
    state = attend(state, ((1,),), [l1])
    l2, state = tie(l2, state)
    l3 = shift(l2, "y", -1)
    state = attend(state, ((-2,),), [r2])
    r3, state = tie(r3, state)
    r4 = shift(r3, "y", 1)
    state = attend(state, ((2, -3),), [l2, r3])
    state = attend(state, ((3,),), [l3])
    parts = attend(state, ((-4,),), [r4], last=True)
    mine = exchange(parts, OCT)
    (shares,) = call(
        merge_kernel,
        [sm, vm, vm, vm, vm],
        [((peers, samples * tok_dev, width), BF16)],
        pos,
        mine,
        gate,
        weights,
        weights_other,
    )
    summands = exchange(shares, "z")
    (update,) = call(sum_kernel, [vm], [((samples * tok_dev, width), BF16)], summands)
    return update.reshape(samples, tok_dev, width)


def solution(mesh):
    fine = Mesh(np.asarray(mesh.devices).reshape(SIZES), AXES)
    blk = ("y", "xlo", "core")
    in_specs = (
        P(None, AXES, None),
        P(AXES),
        P(),
        P(),
        P(),
        P(None, HEADS),
        P(HEADS, blk, None),
        P(HEADS, None),
    )
    return jax.shard_map(body, mesh=fine, in_specs=in_specs, out_specs=P(None, AXES, None), check_vma=False)
```

```python
import functools

import jax
import jax.numpy as jnp
import numpy as np
from jax import lax
from jax.experimental import pallas as pl
from jax.experimental.pallas import tpu as pltpu
from jax.sharding import Mesh
from jax.sharding import PartitionSpec as P

HD = 48
AXES = ("y", "xlo", "core", "z", "xhi")
SIZES = (8, 2, 2, 8, 2)
HEADS = ("z", "xhi")
OCT = ("xlo", "core", "xhi")
F32, BF16 = jnp.float32, jnp.bfloat16
MIB = 1024 * 1024


def params(mib=16):
    return pltpu.CompilerParams(vmem_limit_bytes=mib * MIB)


def dot(a, b, da, db):
    return lax.dot_general(a, b, (((da,), (db,)), ((), ())), preferred_element_type=F32)


def norm_kernel(pos_ref, chain_ref, hot_ref, tok_ref, emb_ref, hemb_ref, out_ref):
    samples, tok_dev, width = tok_ref.shape
    first = pos_ref[0]
    emb = emb_ref[...].astype(F32)
    hemb = hemb_ref[...].astype(F32).reshape(1, width)
    row_of = lax.broadcasted_iota(jnp.int32, (tok_dev, width), 0)
    cond = jnp.zeros((tok_dev, width), F32)
    for t in range(tok_dev):
        chain = chain_ref[t]
        row = jnp.zeros((1, width), F32)
        for c in range(emb_ref.shape[0]):
            row = row + jnp.where(chain == c, 1.0, 0.0) * emb[c : c + 1]
        hits = jnp.int32(0)
        for i in range(hot_ref.shape[0]):
            hits = hits + jnp.where(hot_ref[i] == first + t, 1, 0)
        row = row + jnp.where(hits > 0, 1.0, 0.0) * hemb
        cond = cond + jnp.where(row_of == t, row, 0.0)
    shifted = tok_ref[...].astype(F32) + cond[None]
    average = jnp.mean(shifted, axis=-1, keepdims=True)
    centred = shifted - average
    spread = jnp.mean(centred * centred, axis=-1, keepdims=True)
    normed = (centred * lax.rsqrt(spread + 1e-05)).reshape(samples * tok_dev, width).astype(BF16)
    for g in range(out_ref.shape[0]):
        out_ref[g] = normed


def bias_kernel(pos_ref, b_ref, keep_ref, away_ref, rows_ref):
    xlo, core, xhi = pos_ref[1], pos_ref[2], pos_ref[3]
    row = lax.broadcasted_iota(jnp.int32, (128, 128), 0)
    col = lax.broadcasted_iota(jnp.int32, (128, 128), 1)
    z, t = (row % 64) // 8, row % 8
    from_q = (z * 2 + row // 64) * 8 + t
    from_k = (z * 2 + jnp.bitwise_xor(row // 64, xhi)) * 8 + t
    pick_q = jnp.where(col == from_q, 1.0, 0.0).astype(BF16)
    pick_k = jnp.where(col == from_k, 1.0, 0.0).astype(BF16)
    for b in range(32):
        rows_ref[b] = dot(pick_q, b_ref[0, :, b * 128 : (b + 1) * 128], 1, 0).astype(BF16)
    for role in range(2):
        xl = jnp.bitwise_xor(xlo, role)
        for y in range(8):
            at = (y * 2 + xl) * 2
            keep_ref[role, y] = dot(pick_k, rows_ref[at + core], 1, 1).astype(BF16)
            away_ref[role, y] = dot(pick_k, rows_ref[at + 1 - core], 1, 1).astype(BF16)


def proj_kernel(pos_ref, x_ref, own_ref, other_ref, q_ref, kv_own_ref, kv_other_ref, gate_ref):
    peers, rows, width = x_ref.shape
    pairs = kv_own_ref.shape[0]
    tok = rows // (2 * pairs)
    xhi = pos_ref[3]
    x = x_ref[...].reshape(peers * rows, width)
    for role, w_ref in enumerate((own_ref, other_ref)):
        kv_ref = (kv_own_ref, kv_other_ref)[role]
        full = dot(x, w_ref[: 4 * HD], 1, 1).reshape(peers, 2 * pairs, tok, 4 * HD)
        for p in range(pairs):
            two = jnp.concatenate([full[:, 2 * p + i].reshape(peers * tok, 4 * HD) for i in range(2)], axis=0)
            turned = jnp.transpose(two)
            queries = (turned[:HD] * (1.0 / HD**0.5)).astype(BF16)
            for d in range(4):
                q_ref[2 * d + jnp.bitwise_xor(xhi, role), p] = queries
            kv_ref[p] = turned[HD : 3 * HD].astype(BF16)
            gate_ref[jnp.bitwise_xor(xhi, role), p] = jax.nn.sigmoid(turned[3 * HD :])


def join(a, b):
    lane = lax.broadcasted_iota(jnp.int32, a.shape, 1)
    return jnp.where(lane < 64, a, pltpu.roll(b, 64, 1)), jnp.where(lane < 64, pltpu.roll(a, 64, 1), b)


def join_kernel(own_ref, other_ref, kv_ref):
    for p in range(own_ref.shape[0]):
        even, odd = join(own_ref[p].astype(F32), other_ref[p].astype(F32))
        kv_ref[2 * p] = even.astype(BF16)
        kv_ref[2 * p + 1] = odd.astype(BF16)


def join_q_kernel(pos_ref, q_ref, out_ref):
    me = pos_ref[1] * 2 + pos_ref[2]
    for role in range(4):
        d = 2 * jnp.bitwise_xor(me, role)
        for p in range(q_ref.shape[1]):
            even, odd = join(q_ref[d, p].astype(F32), q_ref[d + 1, p].astype(F32))
            out_ref[2 * p, :, role * 128 : (role + 1) * 128] = even.astype(BF16)
            out_ref[2 * p + 1, :, role * 128 : (role + 1) * 128] = odd.astype(BF16)


def attend_kernel(shifts, pos_ref, q_ref, keep_ref, recv_ref, far_ref, *refs):
    kv_refs, out_ref = refs[:-1], refs[-1]
    me, yy = pos_ref[1] * 2 + pos_ref[2], pos_ref[4]
    row = lax.broadcasted_iota(jnp.int32, (16, 128), 0)
    bias = []
    for by in shifts:
        y = lax.rem(yy + 8 + by, 8)
        bias.append(jnp.concatenate([keep_ref[0, y], recv_ref[0, y], far_ref[0, y], far_ref[1, y]], axis=1).astype(F32))
    bias = jnp.concatenate(bias, axis=0)
    acc, top = [], []
    for i in range(2):
        keys = jnp.concatenate([jnp.transpose(r[i, :HD].astype(F32)).astype(BF16) for r in kv_refs], axis=0)
        vals = jnp.concatenate([r[i, HD:] for r in kv_refs], axis=1)
        vals = jnp.concatenate([vals, jnp.ones((16, vals.shape[1]), BF16)], axis=0)
        scores = jnp.dot(keys, q_ref[i], preferred_element_type=F32) + bias
        best = jnp.max(scores, axis=0, keepdims=True)
        probs = jnp.exp(scores - best).astype(BF16)
        acc.append(jnp.dot(vals, probs, preferred_element_type=F32))
        top.append(best)
    for role in range(4):
        d = 2 * jnp.bitwise_xor(me, role)
        tiles = []
        for i in range(2):
            mine = acc[i][:, role * 128 : (role + 1) * 128]
            total = mine[HD : HD + 1]
            lse = top[i][:, role * 128 : (role + 1) * 128] + jnp.log(total)
            hi = lse.astype(BF16).astype(F32)
            mid = (lse - hi).astype(BF16).astype(F32)
            low = lse - hi - mid
            tail = jnp.where(row == 0, hi, jnp.where(row == 1, mid, jnp.where(row == 2, low, 0.0)))
            tiles.append(jnp.concatenate([mine[:HD] / total, tail], axis=0))
        even, odd = join(tiles[0], tiles[1])
        out_ref[d, 0] = even.astype(BF16)
        out_ref[d + 1, 0] = odd.astype(BF16)


def merge_kernel(pos_ref, p_ref, gate_ref, out_ref):
    core = pos_ref[2]
    peers = out_ref.shape[0]
    tok = 64 // peers
    for p in range(p_ref.shape[1]):
        gated = []
        for other in range(2):
            h = jnp.bitwise_xor(core, other)
            rows = [p_ref[2 * i + h, p].astype(F32) for i in range(4)]
            lse = [r[HD : HD + 1] + r[HD + 1 : HD + 2] + r[HD + 2 : HD + 3] for r in rows]
            top = functools.reduce(jnp.maximum, lse)
            weight = [jnp.exp(v - top) for v in lse]
            gated.append(sum(w * r[:HD] for w, r in zip(weight, rows)) / sum(weight) * gate_ref[h, p])
        turned = jnp.transpose(jnp.concatenate(gated + [jnp.zeros((128 - 2 * HD, 128), F32)], axis=0))
        split = turned.reshape(2, peers, tok, 128)
        for g in range(peers):
            both = jnp.concatenate([split[0, g], split[1, g]], axis=0)
            out_ref[g, 2 * tok * p : 2 * tok * (p + 1)] = both.astype(BF16)


def out_kernel(g_ref, w_near_ref, w_far_ref, out_ref):
    total = None
    for g in range(g_ref.shape[0]):
        gated = g_ref[g]
        term = jnp.dot(gated[:, :HD], w_near_ref[g], preferred_element_type=F32)
        term = term + jnp.dot(gated[:, HD : 2 * HD], w_far_ref[g], preferred_element_type=F32)
        total = term if total is None else total + term
    out_ref[...] = total.astype(BF16)


def shift(x, axis, by):
    n = SIZES[AXES.index(axis)]
    return lax.ppermute(x, axis, [(i, (i + by) % n) for i in range(n)])


def body(tokens, chain_id, hotspots, chain_embed, hot_embed, w_proj, pair_bias, w_out):
    samples, tok_dev, width = tokens.shape
    pairs, peers = samples // 2, 8
    at = {a: lax.axis_index(a) for a in AXES}
    first = ((((at["y"] * 2 + at["xlo"]) * 2 + at["core"]) * 8 + at["z"]) * 2 + at["xhi"]) * tok_dev
    pos = jnp.stack([first, at["xlo"], at["core"], at["xhi"], at["y"]])
    vm = pl.BlockSpec(memory_space=pltpu.VMEM)
    sm = pl.BlockSpec(memory_space=pltpu.SMEM)

    def call(kernel, specs, out, *args, scratch=()):
        shapes = [jax.ShapeDtypeStruct(s, t) for s, t in out]
        return pl.pallas_call(
            kernel,
            out_shape=shapes,
            in_specs=specs,
            out_specs=[vm] * len(out),
            scratch_shapes=scratch,
            compiler_params=params(),
        )(*args)

    def exchange(x, axes):
        return lax.all_to_all(x, axes, split_axis=0, concat_axis=0, tiled=True)

    weights = jnp.concatenate([jnp.transpose(w_proj), w_out], axis=0)
    weights_other = shift(weights, "xhi", 1)
    keep, away = call(
        bias_kernel,
        [sm, vm],
        [((2, 8, 128, 128), BF16)] * 2,
        pos,
        pair_bias,
        scratch=[pltpu.VMEM((32, 128, 128), BF16)],
    )
    recv = shift(away, "core", 1)
    far_out = jnp.stack([keep[1], recv[1]])

    (copies,) = call(
        norm_kernel,
        [sm, sm, sm, vm, vm, vm],
        [((peers, samples * tok_dev, width), BF16)],
        pos,
        chain_id,
        hotspots,
        tokens,
        chain_embed,
        hot_embed,
    )
    gathered = exchange(copies, "z")
    weights_other, far_out = lax.optimization_barrier((weights_other, far_out))
    far = shift(far_out, "xlo", 1)
    gathered, far_out = lax.optimization_barrier((gathered, far_out))
    q_out, kv_own, kv_other, gate = call(
        proj_kernel,
        [sm, vm, vm, vm],
        [
            ((8, pairs, HD, 128), BF16),
            ((pairs, 2 * HD, 128), BF16),
            ((pairs, 2 * HD, 128), BF16),
            ((2, pairs, HD, 128), F32),
        ],
        pos,
        gathered,
        weights,
        weights_other,
    )
    kv_other = shift(kv_other, "xhi", 1)
    (kv,) = call(join_kernel, [vm, vm], [((samples, 2 * HD, 128), BF16)], kv_own, kv_other)

    kv, far = lax.optimization_barrier((kv, far))
    right, left, ring, shifts = kv, kv, [kv], [0]
    for step in range(1, 5):
        right = shift(right, "y", 1)
        if step == 1:
            right, q_out = lax.optimization_barrier((right, q_out))
        ring.append(right)
        shifts.append(-step)
        if step < 4:
            left = shift(left, "y", -1)
            ring.append(left)
            shifts.append(step)
    q_in = exchange(q_out, OCT)
    (q_all,) = call(join_q_kernel, [sm, vm], [((samples, HD, 512), BF16)], pos, q_in)

    w_rows = jnp.where(at["core"] == at["xhi"], w_out, weights_other[4 * HD :])
    w_rows, q_in = lax.optimization_barrier((w_rows, q_in))
    w_near = exchange(jnp.broadcast_to(w_rows[None], (peers, HD, width)), "z")

    def two(*dims):
        return pl.BlockSpec((2,) + dims, lambda s, _: (s,) + (0,) * len(dims))

    whole = pl.BlockSpec((2, 8, 128, 128), lambda s, _: (0, 0, 0, 0))
    parts = pl.pallas_call(
        functools.partial(attend_kernel, tuple(shifts)),
        out_shape=jax.ShapeDtypeStruct((8, pairs, 64, 128), BF16),
        grid_spec=pltpu.PrefetchScalarGridSpec(
            num_scalar_prefetch=1,
            grid=(pairs,),
            in_specs=[two(HD, 512), whole, whole, whole] + [two(2 * HD, 128)] * 8,
            out_specs=pl.BlockSpec((8, 1, 64, 128), lambda s, _: (0, s, 0, 0)),
        ),
        compiler_params=params(32),
        cost_estimate=pl.CostEstimate(flops=1 << 33, bytes_accessed=4 << 20, transcendentals=1 << 22),
    )(pos, q_all, keep, recv, far, *ring)
    parts, w_near = lax.optimization_barrier((parts, w_near))
    w_far = shift(w_near, "core", 1)
    mine = exchange(parts, OCT)
    (gated,) = call(
        merge_kernel, [sm, vm, vm], [((peers, samples * tok_dev, 128), BF16)], pos, mine, gate
    )
    (update,) = call(
        out_kernel, [vm, vm, vm], [((samples * tok_dev, width), BF16)], exchange(gated, "z"), w_near, w_far
    )
    return update.reshape(samples, tok_dev, width)


def solution(mesh):
    fine = Mesh(np.asarray(mesh.devices).reshape(SIZES), AXES)
    blk = ("y", "xlo", "core")
    in_specs = (
        P(None, AXES, None),
        P(AXES),
        P(),
        P(),
        P(),
        P(None, HEADS),
        P(HEADS, blk, None),
        P(HEADS, None),
    )
    return jax.shard_map(body, mesh=fine, in_specs=in_specs, out_specs=P(None, AXES, None), check_vma=False)
```

```python
import functools

import jax
import jax.numpy as jnp
import numpy as np
from jax import lax
from jax.experimental import pallas as pl
from jax.experimental.pallas import tpu as pltpu
from jax.sharding import Mesh
from jax.sharding import PartitionSpec as P

HD = 48
AXES = ("y", "xlo", "core", "z", "xhi")
SIZES = (8, 2, 2, 8, 2)
HEADS = ("z", "xhi")
OCT = ("xlo", "core", "xhi")
F32, BF16 = jnp.float32, jnp.bfloat16
MIB = 1024 * 1024


def params(mib=16):
    return pltpu.CompilerParams(vmem_limit_bytes=mib * MIB)


def dot(a, b, da, db):
    return lax.dot_general(a, b, (((da,), (db,)), ((), ())), preferred_element_type=F32)


def norm_kernel(pos_ref, chain_ref, hot_ref, tok_ref, emb_ref, hemb_ref, out_ref):
    samples, tok_dev, width = tok_ref.shape
    first = pos_ref[0]
    emb = emb_ref[...].astype(F32)
    hemb = hemb_ref[...].astype(F32).reshape(1, width)
    row_of = lax.broadcasted_iota(jnp.int32, (tok_dev, width), 0)
    cond = jnp.zeros((tok_dev, width), F32)
    for t in range(tok_dev):
        chain = chain_ref[t]
        row = jnp.zeros((1, width), F32)
        for c in range(emb_ref.shape[0]):
            row = row + jnp.where(chain == c, 1.0, 0.0) * emb[c : c + 1]
        hits = jnp.int32(0)
        for i in range(hot_ref.shape[0]):
            hits = hits + jnp.where(hot_ref[i] == first + t, 1, 0)
        row = row + jnp.where(hits > 0, 1.0, 0.0) * hemb
        cond = cond + jnp.where(row_of == t, row, 0.0)
    shifted = tok_ref[...].astype(F32) + cond[None]
    average = jnp.mean(shifted, axis=-1, keepdims=True)
    centred = shifted - average
    spread = jnp.mean(centred * centred, axis=-1, keepdims=True)
    normed = (centred * lax.rsqrt(spread + 1e-05)).reshape(samples * tok_dev, width).astype(BF16)
    for g in range(out_ref.shape[0]):
        out_ref[g] = normed


def bias_kernel(pos_ref, b_ref, keep_ref, away_ref, rows_ref):
    xlo, core, xhi = pos_ref[1], pos_ref[2], pos_ref[3]
    row = lax.broadcasted_iota(jnp.int32, (128, 128), 0)
    col = lax.broadcasted_iota(jnp.int32, (128, 128), 1)
    z, t = (row % 64) // 8, row % 8
    from_q = (z * 2 + row // 64) * 8 + t
    from_k = (z * 2 + jnp.bitwise_xor(row // 64, xhi)) * 8 + t
    pick_q = jnp.where(col == from_q, 1.0, 0.0).astype(BF16)
    pick_k = jnp.where(col == from_k, 1.0, 0.0).astype(BF16)
    for b in range(32):
        rows_ref[b] = dot(pick_q, b_ref[0, :, b * 128 : (b + 1) * 128], 1, 0).astype(BF16)
    for role in range(2):
        xl = jnp.bitwise_xor(xlo, role)
        for y in range(8):
            at = (y * 2 + xl) * 2
            keep_ref[role, y] = dot(pick_k, rows_ref[at + core], 1, 1).astype(BF16)
            away_ref[role, y] = dot(pick_k, rows_ref[at + 1 - core], 1, 1).astype(BF16)


def proj_kernel(pos_ref, x_ref, own_ref, other_ref, q_ref, kv_own_ref, kv_other_ref, gate_ref):
    peers, rows, width = x_ref.shape
    pairs = kv_own_ref.shape[0]
    tok = rows // (2 * pairs)
    xhi = pos_ref[3]
    x = x_ref[...].reshape(peers * rows, width)
    for role, w_ref in enumerate((own_ref, other_ref)):
        kv_ref = (kv_own_ref, kv_other_ref)[role]
        full = dot(x, w_ref[: 4 * HD], 1, 1).reshape(peers, 2 * pairs, tok, 4 * HD)
        for p in range(pairs):
            two = jnp.concatenate([full[:, 2 * p + i].reshape(peers * tok, 4 * HD) for i in range(2)], axis=0)
            turned = jnp.transpose(two)
            queries = (turned[:HD] * (1.0 / HD**0.5)).astype(BF16)
            for d in range(4):
                q_ref[2 * d + jnp.bitwise_xor(xhi, role), p] = queries
            kv_ref[p] = turned[HD : 3 * HD].astype(BF16)
            gate_ref[jnp.bitwise_xor(xhi, role), p] = jax.nn.sigmoid(turned[3 * HD :])


def join(a, b):
    lane = lax.broadcasted_iota(jnp.int32, a.shape, 1)
    return jnp.where(lane < 64, a, pltpu.roll(b, 64, 1)), jnp.where(lane < 64, pltpu.roll(a, 64, 1), b)


def join_kernel(own_ref, other_ref, kv_ref):
    for p in range(own_ref.shape[0]):
        even, odd = join(own_ref[p].astype(F32), other_ref[p].astype(F32))
        kv_ref[2 * p] = even.astype(BF16)
        kv_ref[2 * p + 1] = odd.astype(BF16)


def join_q_kernel(pos_ref, q_ref, out_ref):
    me = pos_ref[1] * 2 + pos_ref[2]
    for role in range(4):
        d = 2 * jnp.bitwise_xor(me, role)
        for p in range(q_ref.shape[1]):
            even, odd = join(q_ref[d, p].astype(F32), q_ref[d + 1, p].astype(F32))
            out_ref[2 * p, :, role * 128 : (role + 1) * 128] = even.astype(BF16)
            out_ref[2 * p + 1, :, role * 128 : (role + 1) * 128] = odd.astype(BF16)


def attend_kernel(steps, first, last, pos_ref, q_ref, keep_ref, recv_ref, far_ref, *refs):
    count = sum(len(s) for s in steps)
    kv_refs, rest = refs[:count], refs[count:]
    me, yy = pos_ref[1] * 2 + pos_ref[2], pos_ref[4]
    acc = [None, None] if first else [rest[0][i] for i in range(2)]
    top = [None, None] if first else [rest[1][i, :1] for i in range(2)]
    at = 0
    for step in steps:
        bias = []
        for sh in step:
            y = lax.rem(yy + 8 + sh, 8)
            bias.append(
                jnp.concatenate([keep_ref[0, y], recv_ref[0, y], far_ref[0, y], far_ref[1, y]], axis=1).astype(F32)
            )
        bias = jnp.concatenate(bias, axis=0)
        blocks = kv_refs[at : at + len(step)]
        at += len(step)
        for i in range(2):
            keys = jnp.concatenate([jnp.transpose(r[i, :HD].astype(F32)).astype(BF16) for r in blocks], axis=0)
            vals = jnp.concatenate([r[i, HD:] for r in blocks], axis=1)
            vals = jnp.concatenate([vals, jnp.ones((16, vals.shape[1]), BF16)], axis=0)
            scores = jnp.dot(keys, q_ref[i], preferred_element_type=F32) + bias
            best = jnp.max(scores, axis=0, keepdims=True)
            if top[i] is not None:
                best = jnp.maximum(best, top[i])
            probs = jnp.exp(scores - best).astype(BF16)
            part = jnp.dot(vals, probs, preferred_element_type=F32)
            if top[i] is not None:
                part = part + acc[i] * jnp.exp(top[i] - best)
            acc[i], top[i] = part, best
    if not last:
        for i in range(2):
            rest[-2][i] = acc[i]
            rest[-1][i] = jnp.broadcast_to(top[i], (8, top[i].shape[1]))
        return
    out_ref = rest[-1]
    row = lax.broadcasted_iota(jnp.int32, (16, 128), 0)
    for role in range(4):
        d = 2 * jnp.bitwise_xor(me, role)
        tiles = []
        for i in range(2):
            mine = acc[i][:, role * 128 : (role + 1) * 128]
            total = mine[HD : HD + 1]
            lse = top[i][:, role * 128 : (role + 1) * 128] + jnp.log(total)
            hi = lse.astype(BF16).astype(F32)
            mid = (lse - hi).astype(BF16).astype(F32)
            low = lse - hi - mid
            tail = jnp.where(row == 0, hi, jnp.where(row == 1, mid, jnp.where(row == 2, low, 0.0)))
            tiles.append(jnp.concatenate([mine[:HD] / total, tail], axis=0))
        even, odd = join(tiles[0], tiles[1])
        out_ref[d, 0] = even.astype(BF16)
        out_ref[d + 1, 0] = odd.astype(BF16)


def merge_kernel(pos_ref, p_ref, gate_ref, out_ref):
    core = pos_ref[2]
    peers = out_ref.shape[0]
    tok = 64 // peers
    for p in range(p_ref.shape[1]):
        gated = []
        for other in range(2):
            h = jnp.bitwise_xor(core, other)
            rows = [p_ref[2 * i + h, p].astype(F32) for i in range(4)]
            lse = [r[HD : HD + 1] + r[HD + 1 : HD + 2] + r[HD + 2 : HD + 3] for r in rows]
            top = functools.reduce(jnp.maximum, lse)
            weight = [jnp.exp(v - top) for v in lse]
            gated.append(sum(w * r[:HD] for w, r in zip(weight, rows)) / sum(weight) * gate_ref[h, p])
        turned = jnp.transpose(jnp.concatenate(gated + [jnp.zeros((128 - 2 * HD, 128), F32)], axis=0))
        split = turned.reshape(2, peers, tok, 128)
        for g in range(peers):
            both = jnp.concatenate([split[0, g], split[1, g]], axis=0)
            out_ref[g, 2 * tok * p : 2 * tok * (p + 1)] = both.astype(BF16)


def out_kernel(g_ref, w_near_ref, w_far_ref, out_ref):
    total = None
    for g in range(g_ref.shape[0]):
        gated = g_ref[g]
        term = jnp.dot(gated[:, :HD], w_near_ref[g], preferred_element_type=F32)
        term = term + jnp.dot(gated[:, HD : 2 * HD], w_far_ref[g], preferred_element_type=F32)
        total = term if total is None else total + term
    out_ref[...] = total.astype(BF16)


def shift(x, axis, by):
    n = SIZES[AXES.index(axis)]
    return lax.ppermute(x, axis, [(i, (i + by) % n) for i in range(n)])


def body(tokens, chain_id, hotspots, chain_embed, hot_embed, w_proj, pair_bias, w_out):
    samples, tok_dev, width = tokens.shape
    pairs, peers = samples // 2, 8
    at = {a: lax.axis_index(a) for a in AXES}
    first = ((((at["y"] * 2 + at["xlo"]) * 2 + at["core"]) * 8 + at["z"]) * 2 + at["xhi"]) * tok_dev
    pos = jnp.stack([first, at["xlo"], at["core"], at["xhi"], at["y"]])
    vm = pl.BlockSpec(memory_space=pltpu.VMEM)
    sm = pl.BlockSpec(memory_space=pltpu.SMEM)

    def call(kernel, specs, out, *args, scratch=(), mib=16):
        shapes = [jax.ShapeDtypeStruct(s, t) for s, t in out]
        return pl.pallas_call(
            kernel,
            out_shape=shapes,
            in_specs=specs,
            out_specs=[vm] * len(out),
            scratch_shapes=scratch,
            compiler_params=params(mib),
        )(*args)

    def exchange(x, axes):
        return lax.all_to_all(x, axes, split_axis=0, concat_axis=0, tiled=True)

    weights = jnp.concatenate([jnp.transpose(w_proj), w_out], axis=0)
    weights_other = shift(weights, "xhi", 1)
    keep, away = call(
        bias_kernel,
        [sm, vm],
        [((2, 8, 128, 128), BF16)] * 2,
        pos,
        pair_bias,
        scratch=[pltpu.VMEM((32, 128, 128), BF16)],
    )
    recv = shift(away, "core", 1)
    far_out = jnp.stack([keep[1], recv[1]])

    (copies,) = call(
        norm_kernel,
        [sm, sm, sm, vm, vm, vm],
        [((peers, samples * tok_dev, width), BF16)],
        pos,
        chain_id,
        hotspots,
        tokens,
        chain_embed,
        hot_embed,
        mib=56,
    )
    gathered = exchange(copies, "z")
    weights_other, far_out = lax.optimization_barrier((weights_other, far_out))
    far = shift(far_out, "xlo", 1)
    gathered, far_out = lax.optimization_barrier((gathered, far_out))
    q_out, kv_own, kv_other, gate = call(
        proj_kernel,
        [sm, vm, vm, vm],
        [
            ((8, pairs, HD, 128), BF16),
            ((pairs, 2 * HD, 128), BF16),
            ((pairs, 2 * HD, 128), BF16),
            ((2, pairs, HD, 128), F32),
        ],
        pos,
        gathered,
        weights,
        weights_other,
    )
    w_rows = jnp.where(at["core"] == at["xhi"], w_out, weights_other[4 * HD :])
    w_near = jnp.broadcast_to(w_rows[None], (peers, HD, width))
    w_near, kv_own = lax.optimization_barrier((w_near, kv_own))
    w_near = exchange(w_near, "z")
    kv_other = shift(kv_other, "xhi", 1)
    (kv,) = call(join_kernel, [vm, vm], [((samples, 2 * HD, 128), BF16)], kv_own, kv_other)

    right, left, ring, shifts = kv, kv, [kv], [0]
    for step in range(1, 5):
        right = shift(right, "y", 1)
        ring.append(right)
        shifts.append(-step)
        if step < 4:
            left = shift(left, "y", -1)
            if step == 1:
                left, q_out, w_near = lax.optimization_barrier((left, q_out, w_near))
            ring.append(left)
            shifts.append(step)
    q_in = exchange(q_out, OCT)
    (q_all,) = call(join_q_kernel, [sm, vm], [((samples, HD, 512), BF16)], pos, q_in)

    def two(*dims):
        return pl.BlockSpec((2,) + dims, lambda s, _: (s,) + (0,) * len(dims))

    whole = pl.BlockSpec((2, 8, 128, 128), lambda s, _: (0, 0, 0, 0))
    state = (((samples, 64, 512), F32), ((samples, 8, 512), F32))

    def attend(blocks, carried, last):
        out = [((8, pairs, 64, 128), BF16)] if last else state
        state_specs = [two(64, 512), two(8, 512)]
        return pl.pallas_call(
            functools.partial(attend_kernel, (tuple(shifts[i] for i in blocks),), not carried, last),
            out_shape=[jax.ShapeDtypeStruct(s, t) for s, t in out],
            grid_spec=pltpu.PrefetchScalarGridSpec(
                num_scalar_prefetch=1,
                grid=(pairs,),
                in_specs=[two(HD, 512), whole, whole, whole]
                + [two(2 * HD, 128)] * len(blocks)
                + (state_specs if carried else []),
                out_specs=[pl.BlockSpec((8, 1, 64, 128), lambda s, _: (0, s, 0, 0))] if last else state_specs,
            ),
            compiler_params=params(24),
            cost_estimate=pl.CostEstimate(
                flops=len(blocks) << 30, bytes_accessed=4 << 20, transcendentals=len(blocks) << 19
            ),
        )(pos, q_all, keep, recv, far, *[ring[i] for i in blocks], *carried)

    carried = attend((0, 1, 2, 3, 4, 5), [], False)
    (parts,) = attend((6, 7), carried, True)
    parts, w_near = lax.optimization_barrier((parts, w_near))
    w_far = shift(w_near, "core", 1)
    mine = exchange(parts, OCT)
    (gated,) = call(
        merge_kernel, [sm, vm, vm], [((peers, samples * tok_dev, 128), BF16)], pos, mine, gate
    )
    (update,) = call(
        out_kernel, [vm, vm, vm], [((samples * tok_dev, width), BF16)], exchange(gated, "z"), w_near, w_far
    )
    return update.reshape(samples, tok_dev, width)


def solution(mesh):
    fine = Mesh(np.asarray(mesh.devices).reshape(SIZES), AXES)
    blk = ("y", "xlo", "core")
    in_specs = (
        P(None, AXES, None),
        P(AXES),
        P(),
        P(),
        P(),
        P(None, HEADS),
        P(HEADS, blk, None),
        P(HEADS, None),
    )
    return jax.shard_map(body, mesh=fine, in_specs=in_specs, out_specs=P(None, AXES, None), check_vma=False)
```

```python
import functools

import jax
import jax.numpy as jnp
import numpy as np
from jax import lax
from jax.experimental import pallas as pl
from jax.experimental.pallas import tpu as pltpu
from jax.sharding import Mesh
from jax.sharding import PartitionSpec as P

HD = 48
AXES = ("y", "xlo", "core", "z", "xhi")
SIZES = (8, 2, 2, 8, 2)
HEADS = ("z", "xhi")
OCT = ("xlo", "core", "xhi")
F32, BF16 = jnp.float32, jnp.bfloat16
MIB = 1024 * 1024


def params(mib=16):
    return pltpu.CompilerParams(vmem_limit_bytes=mib * MIB)


def dot(a, b, da, db):
    return lax.dot_general(a, b, (((da,), (db,)), ((), ())), preferred_element_type=F32)


def norm_kernel(pos_ref, chain_ref, hot_ref, tok_ref, emb_ref, hemb_ref, out_ref):
    samples, tok_dev, width = tok_ref.shape
    first = pos_ref[0]
    emb = emb_ref[...].astype(F32)
    hemb = hemb_ref[...].astype(F32).reshape(1, width)
    row_of = lax.broadcasted_iota(jnp.int32, (tok_dev, width), 0)
    cond = jnp.zeros((tok_dev, width), F32)
    for t in range(tok_dev):
        chain = chain_ref[t]
        row = jnp.zeros((1, width), F32)
        for c in range(emb_ref.shape[0]):
            row = row + jnp.where(chain == c, 1.0, 0.0) * emb[c : c + 1]
        hits = jnp.int32(0)
        for i in range(hot_ref.shape[0]):
            hits = hits + jnp.where(hot_ref[i] == first + t, 1, 0)
        row = row + jnp.where(hits > 0, 1.0, 0.0) * hemb
        cond = cond + jnp.where(row_of == t, row, 0.0)
    shifted = tok_ref[...].astype(F32) + cond[None]
    average = jnp.mean(shifted, axis=-1, keepdims=True)
    centred = shifted - average
    spread = jnp.mean(centred * centred, axis=-1, keepdims=True)
    normed = (centred * lax.rsqrt(spread + 1e-05)).reshape(samples * tok_dev, width).astype(BF16)
    for g in range(out_ref.shape[0]):
        out_ref[g] = normed


def bias_kernel(pos_ref, b_ref, keep_ref, away_ref, rows_ref):
    xlo, core, xhi = pos_ref[1], pos_ref[2], pos_ref[3]
    row = lax.broadcasted_iota(jnp.int32, (128, 128), 0)
    col = lax.broadcasted_iota(jnp.int32, (128, 128), 1)
    z, t = (row % 64) // 8, row % 8
    from_q = (z * 2 + row // 64) * 8 + t
    from_k = (z * 2 + jnp.bitwise_xor(row // 64, xhi)) * 8 + t
    pick_q = jnp.where(col == from_q, 1.0, 0.0).astype(BF16)
    pick_k = jnp.where(col == from_k, 1.0, 0.0).astype(BF16)
    for b in range(32):
        rows_ref[b] = dot(pick_q, b_ref[0, :, b * 128 : (b + 1) * 128], 1, 0).astype(BF16)
    for role in range(2):
        xl = jnp.bitwise_xor(xlo, role)
        for y in range(8):
            at = (y * 2 + xl) * 2
            keep_ref[role, y] = dot(pick_k, rows_ref[at + core], 1, 1).astype(BF16)
            away_ref[role, y] = dot(pick_k, rows_ref[at + 1 - core], 1, 1).astype(BF16)


def proj_kernel(pos_ref, x_ref, own_ref, other_ref, q_ref, kv_own_ref, kv_other_ref, gate_ref):
    peers, rows, width = x_ref.shape
    pairs = kv_own_ref.shape[0]
    tok = rows // (2 * pairs)
    xhi = pos_ref[3]
    x = x_ref[...].reshape(peers * rows, width)
    for role, w_ref in enumerate((own_ref, other_ref)):
        kv_ref = (kv_own_ref, kv_other_ref)[role]
        full = dot(x, w_ref[: 4 * HD], 1, 1).reshape(peers, 2 * pairs, tok, 4 * HD)
        for p in range(pairs):
            two = jnp.concatenate([full[:, 2 * p + i].reshape(peers * tok, 4 * HD) for i in range(2)], axis=0)
            turned = jnp.transpose(two)
            queries = (turned[:HD] * (1.0 / HD**0.5)).astype(BF16)
            for d in range(4):
                q_ref[2 * d + jnp.bitwise_xor(xhi, role), p] = queries
            kv_ref[p] = turned[HD : 3 * HD].astype(BF16)
            gate_ref[jnp.bitwise_xor(xhi, role), p] = jax.nn.sigmoid(turned[3 * HD :])


def join(a, b):
    lane = lax.broadcasted_iota(jnp.int32, a.shape, 1)
    return jnp.where(lane < 64, a, pltpu.roll(b, 64, 1)), jnp.where(lane < 64, pltpu.roll(a, 64, 1), b)


def join_kernel(own_ref, other_ref, kv_ref):
    for p in range(own_ref.shape[0]):
        even, odd = join(own_ref[p].astype(F32), other_ref[p].astype(F32))
        kv_ref[2 * p] = even.astype(BF16)
        kv_ref[2 * p + 1] = odd.astype(BF16)


def join_q_kernel(pos_ref, q_ref, out_ref):
    me = pos_ref[1] * 2 + pos_ref[2]
    for role in range(4):
        d = 2 * jnp.bitwise_xor(me, role)
        for p in range(q_ref.shape[1]):
            even, odd = join(q_ref[d, p].astype(F32), q_ref[d + 1, p].astype(F32))
            out_ref[2 * p, :, role * 128 : (role + 1) * 128] = even.astype(BF16)
            out_ref[2 * p + 1, :, role * 128 : (role + 1) * 128] = odd.astype(BF16)


def attend_kernel(steps, first, last, pos_ref, q_ref, keep_ref, recv_ref, far_ref, *refs):
    count = sum(len(s) for s in steps)
    kv_refs, rest = refs[:count], refs[count:]
    me, yy = pos_ref[1] * 2 + pos_ref[2], pos_ref[4]
    acc = [None, None] if first else [rest[0][i] for i in range(2)]
    top = [None, None] if first else [rest[1][i, :1] for i in range(2)]
    at = 0
    for step in steps:
        bias = []
        for sh in step:
            y = lax.rem(yy + 8 + sh, 8)
            bias.append(
                jnp.concatenate([keep_ref[0, y], recv_ref[0, y], far_ref[0, y], far_ref[1, y]], axis=1).astype(F32)
            )
        bias = jnp.concatenate(bias, axis=0)
        blocks = kv_refs[at : at + len(step)]
        at += len(step)
        for i in range(2):
            keys = jnp.concatenate([jnp.transpose(r[i, :HD].astype(F32)).astype(BF16) for r in blocks], axis=0)
            vals = jnp.concatenate([r[i, HD:] for r in blocks], axis=1)
            vals = jnp.concatenate([vals, jnp.ones((16, vals.shape[1]), BF16)], axis=0)
            scores = jnp.dot(keys, q_ref[i], preferred_element_type=F32) + bias
            best = jnp.max(scores, axis=0, keepdims=True)
            if top[i] is not None:
                best = jnp.maximum(best, top[i])
            probs = jnp.exp(scores - best).astype(BF16)
            part = jnp.dot(vals, probs, preferred_element_type=F32)
            if top[i] is not None:
                part = part + acc[i] * jnp.exp(top[i] - best)
            acc[i], top[i] = part, best
    if not last:
        for i in range(2):
            rest[-2][i] = acc[i]
            rest[-1][i] = jnp.broadcast_to(top[i], (8, top[i].shape[1]))
        return
    out_ref = rest[-1]
    row = lax.broadcasted_iota(jnp.int32, (16, 128), 0)
    for role in range(4):
        d = 2 * jnp.bitwise_xor(me, role)
        tiles = []
        for i in range(2):
            mine = acc[i][:, role * 128 : (role + 1) * 128]
            total = mine[HD : HD + 1]
            lse = top[i][:, role * 128 : (role + 1) * 128] + jnp.log(total)
            hi = lse.astype(BF16).astype(F32)
            mid = (lse - hi).astype(BF16).astype(F32)
            low = lse - hi - mid
            tail = jnp.where(row == 0, hi, jnp.where(row == 1, mid, jnp.where(row == 2, low, 0.0)))
            tiles.append(jnp.concatenate([mine[:HD] / total, tail], axis=0))
        even, odd = join(tiles[0], tiles[1])
        out_ref[d, 0] = even.astype(BF16)
        out_ref[d + 1, 0] = odd.astype(BF16)


def merge_kernel(pos_ref, p_ref, gate_ref, out_ref):
    core = pos_ref[2]
    peers = out_ref.shape[0]
    tok = 64 // peers
    for p in range(p_ref.shape[1]):
        gated = []
        for other in range(2):
            h = jnp.bitwise_xor(core, other)
            rows = [p_ref[2 * i + h, p].astype(F32) for i in range(4)]
            lse = [r[HD : HD + 1] + r[HD + 1 : HD + 2] + r[HD + 2 : HD + 3] for r in rows]
            top = functools.reduce(jnp.maximum, lse)
            weight = [jnp.exp(v - top) for v in lse]
            gated.append(sum(w * r[:HD] for w, r in zip(weight, rows)) / sum(weight) * gate_ref[h, p])
        turned = jnp.transpose(jnp.concatenate(gated + [jnp.zeros((128 - 2 * HD, 128), F32)], axis=0))
        split = turned.reshape(2, peers, tok, 128)
        for g in range(peers):
            both = jnp.concatenate([split[0, g], split[1, g]], axis=0)
            out_ref[g, 2 * tok * p : 2 * tok * (p + 1)] = both.astype(BF16)


def out_kernel(g_ref, w_near_ref, w_far_ref, out_ref):
    total = None
    for g in range(g_ref.shape[0]):
        gated = g_ref[g]
        term = jnp.dot(gated[:, :HD], w_near_ref[g], preferred_element_type=F32)
        term = term + jnp.dot(gated[:, HD : 2 * HD], w_far_ref[g], preferred_element_type=F32)
        total = term if total is None else total + term
    out_ref[...] = total.astype(BF16)


def shift(x, axis, by):
    n = SIZES[AXES.index(axis)]
    return lax.ppermute(x, axis, [(i, (i + by) % n) for i in range(n)])


def body(tokens, chain_id, hotspots, chain_embed, hot_embed, w_proj, pair_bias, w_out):
    samples, tok_dev, width = tokens.shape
    pairs, peers = samples // 2, 8
    at = {a: lax.axis_index(a) for a in AXES}
    first = ((((at["y"] * 2 + at["xlo"]) * 2 + at["core"]) * 8 + at["z"]) * 2 + at["xhi"]) * tok_dev
    pos = jnp.stack([first, at["xlo"], at["core"], at["xhi"], at["y"]])
    vm = pl.BlockSpec(memory_space=pltpu.VMEM)
    sm = pl.BlockSpec(memory_space=pltpu.SMEM)

    def call(kernel, specs, out, *args, scratch=(), mib=16):
        shapes = [jax.ShapeDtypeStruct(s, t) for s, t in out]
        return pl.pallas_call(
            kernel,
            out_shape=shapes,
            in_specs=specs,
            out_specs=[vm] * len(out),
            scratch_shapes=scratch,
            compiler_params=params(mib),
        )(*args)

    def exchange(x, axes):
        return lax.all_to_all(x, axes, split_axis=0, concat_axis=0, tiled=True)

    weights = jnp.concatenate([jnp.transpose(w_proj), w_out], axis=0)
    weights_other = shift(weights, "xhi", 1)
    keep, away = call(
        bias_kernel,
        [sm, vm],
        [((2, 8, 128, 128), BF16)] * 2,
        pos,
        pair_bias,
        scratch=[pltpu.VMEM((32, 128, 128), BF16)],
    )
    recv = shift(away, "core", 1)
    far_out = jnp.stack([keep[1], recv[1]])

    (copies,) = call(
        norm_kernel,
        [sm, sm, sm, vm, vm, vm],
        [((peers, samples * tok_dev, width), BF16)],
        first[None],
        chain_id,
        hotspots,
        tokens,
        chain_embed,
        hot_embed,
        mib=56,
    )
    gathered = exchange(copies, "z")
    w_rows = jnp.where(at["core"] == at["xhi"], w_out, weights_other[4 * HD :])
    w_near = jnp.broadcast_to(w_rows[None], (peers, HD, width))
    far = shift(far_out, "xlo", 1)
    gathered, far_out, w_near = lax.optimization_barrier((gathered, far_out, w_near))
    q_out, kv_own, kv_other, gate = call(
        proj_kernel,
        [sm, vm, vm, vm],
        [
            ((8, pairs, HD, 128), BF16),
            ((pairs, 2 * HD, 128), BF16),
            ((pairs, 2 * HD, 128), BF16),
            ((2, pairs, HD, 128), F32),
        ],
        pos,
        gathered,
        weights,
        weights_other,
    )
    w_near, kv_own, kv_other, far = lax.optimization_barrier((w_near, kv_own, kv_other, far))
    w_near = exchange(w_near, "z")
    kv_other = shift(kv_other, "xhi", 1)
    (kv,) = call(join_kernel, [vm, vm], [((samples, 2 * HD, 128), BF16)], kv_own, kv_other)

    right, left, ring, shifts = kv, kv, [kv], [0]
    for step in range(1, 5):
        right = shift(right, "y", 1)
        ring.append(right)
        shifts.append(-step)
        if step < 4:
            left = shift(left, "y", -1)
            if step == 1:
                left, q_out, w_near = lax.optimization_barrier((left, q_out, w_near))
            ring.append(left)
            shifts.append(step)
    q_in = exchange(q_out, OCT)
    (q_all,) = call(join_q_kernel, [sm, vm], [((samples, HD, 512), BF16)], pos, q_in)

    def two(*dims):
        return pl.BlockSpec((2,) + dims, lambda s, _: (s,) + (0,) * len(dims))

    whole = pl.BlockSpec((2, 8, 128, 128), lambda s, _: (0, 0, 0, 0))
    state = (((samples, 64, 512), F32), ((samples, 8, 512), F32))

    def attend(blocks, carried, last):
        out = [((8, pairs, 64, 128), BF16)] if last else state
        state_specs = [two(64, 512), two(8, 512)]
        return pl.pallas_call(
            functools.partial(attend_kernel, (tuple(shifts[i] for i in blocks),), not carried, last),
            out_shape=[jax.ShapeDtypeStruct(s, t) for s, t in out],
            grid_spec=pltpu.PrefetchScalarGridSpec(
                num_scalar_prefetch=1,
                grid=(pairs,),
                in_specs=[two(HD, 512), whole, whole, whole]
                + [two(2 * HD, 128)] * len(blocks)
                + (state_specs if carried else []),
                out_specs=[pl.BlockSpec((8, 1, 64, 128), lambda s, _: (0, s, 0, 0))] if last else state_specs,
            ),
            compiler_params=params(24),
            cost_estimate=pl.CostEstimate(
                flops=len(blocks) << 30, bytes_accessed=4 << 20, transcendentals=len(blocks) << 19
            ),
        )(pos, q_all, keep, recv, far, *[ring[i] for i in blocks], *carried)

    carried = attend((0, 1, 2, 3, 4, 5), [], False)
    (parts,) = attend((6, 7), carried, True)
    parts, w_near = lax.optimization_barrier((parts, w_near))
    w_far = shift(w_near, "core", 1)
    mine = exchange(parts, OCT)
    (gated,) = call(
        merge_kernel, [sm, vm, vm], [((peers, samples * tok_dev, 128), BF16)], pos, mine, gate
    )
    (update,) = call(
        out_kernel, [vm, vm, vm], [((samples * tok_dev, width), BF16)], exchange(gated, "z"), w_near, w_far
    )
    return update.reshape(samples, tok_dev, width)


def solution(mesh):
    fine = Mesh(np.asarray(mesh.devices).reshape(SIZES), AXES)
    blk = ("y", "xlo", "core")
    in_specs = (
        P(None, AXES, None),
        P(AXES),
        P(),
        P(),
        P(),
        P(None, HEADS),
        P(HEADS, blk, None),
        P(HEADS, None),
    )
    return jax.shard_map(body, mesh=fine, in_specs=in_specs, out_specs=P(None, AXES, None), check_vma=False)
```

```python
import functools

import jax
import jax.numpy as jnp
import numpy as np
from jax import lax
from jax.experimental import pallas as pl
from jax.experimental.pallas import tpu as pltpu
from jax.sharding import Mesh
from jax.sharding import PartitionSpec as P

HD = 48
AXES = ("y", "xlo", "core", "z", "xhi")
SIZES = (8, 2, 2, 8, 2)
HEADS = ("z", "xhi")
OCT = ("xlo", "core", "xhi")
F32, BF16 = jnp.float32, jnp.bfloat16
MIB = 1024 * 1024


def params(mib=16):
    return pltpu.CompilerParams(vmem_limit_bytes=mib * MIB)


def dot(a, b, da, db):
    return lax.dot_general(a, b, (((da,), (db,)), ((), ())), preferred_element_type=F32)


def norm_kernel(pos_ref, chain_ref, hot_ref, tok_ref, emb_ref, hemb_ref, out_ref):
    samples, tok_dev, width = tok_ref.shape
    first = pos_ref[0]
    emb = emb_ref[...].astype(F32)
    hemb = hemb_ref[...].astype(F32).reshape(1, width)
    row_of = lax.broadcasted_iota(jnp.int32, (tok_dev, width), 0)
    cond = jnp.zeros((tok_dev, width), F32)
    for t in range(tok_dev):
        chain = chain_ref[t]
        row = jnp.zeros((1, width), F32)
        for c in range(emb_ref.shape[0]):
            row = row + jnp.where(chain == c, 1.0, 0.0) * emb[c : c + 1]
        hits = jnp.int32(0)
        for i in range(hot_ref.shape[0]):
            hits = hits + jnp.where(hot_ref[i] == first + t, 1, 0)
        row = row + jnp.where(hits > 0, 1.0, 0.0) * hemb
        cond = cond + jnp.where(row_of == t, row, 0.0)
    shifted = tok_ref[...].astype(F32) + cond[None]
    average = jnp.mean(shifted, axis=-1, keepdims=True)
    centred = shifted - average
    spread = jnp.mean(centred * centred, axis=-1, keepdims=True)
    normed = (centred * lax.rsqrt(spread + 1e-05)).reshape(samples * tok_dev, width).astype(BF16)
    for g in range(out_ref.shape[0]):
        out_ref[g] = normed


def bias_kernel(pos_ref, b_ref, keep_ref, away_ref, rows_ref):
    xlo, core, xhi = pos_ref[1], pos_ref[2], pos_ref[3]
    row = lax.broadcasted_iota(jnp.int32, (128, 128), 0)
    col = lax.broadcasted_iota(jnp.int32, (128, 128), 1)
    z, t = (row % 64) // 8, row % 8
    from_q = (z * 2 + row // 64) * 8 + t
    from_k = (z * 2 + jnp.bitwise_xor(row // 64, xhi)) * 8 + t
    pick_q = jnp.where(col == from_q, 1.0, 0.0).astype(BF16)
    pick_k = jnp.where(col == from_k, 1.0, 0.0).astype(BF16)
    for b in range(32):
        rows_ref[b] = dot(pick_q, b_ref[0, :, b * 128 : (b + 1) * 128], 1, 0).astype(BF16)
    for role in range(2):
        xl = jnp.bitwise_xor(xlo, role)
        for y in range(8):
            at = (y * 2 + xl) * 2
            keep_ref[role, y] = dot(pick_k, rows_ref[at + core], 1, 1).astype(BF16)
            away_ref[role, y] = dot(pick_k, rows_ref[at + 1 - core], 1, 1).astype(BF16)


def proj_kernel(pos_ref, x_ref, own_ref, other_ref, q_ref, kv_own_ref, kv_other_ref, gate_ref, w_ref):
    peers, rows, width = x_ref.shape
    pairs = kv_own_ref.shape[0]
    tok = rows // (2 * pairs)
    xhi = pos_ref[3]
    x = x_ref[...].reshape(peers * rows, width)
    for role, in_ref in enumerate((own_ref, other_ref)):
        kv_ref = (kv_own_ref, kv_other_ref)[role]

        @pl.when(jnp.bitwise_xor(pos_ref[2], xhi) == role)
        def _():
            for g in range(peers):
                w_ref[g] = in_ref[4 * HD :]

        full = dot(x, in_ref[: 4 * HD], 1, 1).reshape(peers, 2 * pairs, tok, 4 * HD)
        for p in range(pairs):
            two = jnp.concatenate([full[:, 2 * p + i].reshape(peers * tok, 4 * HD) for i in range(2)], axis=0)
            turned = jnp.transpose(two)
            queries = (turned[:HD] * (1.0 / HD**0.5)).astype(BF16)
            for d in range(4):
                q_ref[2 * d + jnp.bitwise_xor(xhi, role), p] = queries
            kv_ref[p] = turned[HD : 3 * HD].astype(BF16)
            gate_ref[jnp.bitwise_xor(xhi, role), p] = jax.nn.sigmoid(turned[3 * HD :])


def join(a, b):
    lane = lax.broadcasted_iota(jnp.int32, a.shape, 1)
    return jnp.where(lane < 64, a, pltpu.roll(b, 64, 1)), jnp.where(lane < 64, pltpu.roll(a, 64, 1), b)


def join_kernel(own_ref, other_ref, kv_ref):
    for p in range(own_ref.shape[0]):
        even, odd = join(own_ref[p].astype(F32), other_ref[p].astype(F32))
        kv_ref[2 * p] = even.astype(BF16)
        kv_ref[2 * p + 1] = odd.astype(BF16)


def join_q_kernel(pos_ref, q_ref, out_ref):
    me = pos_ref[1] * 2 + pos_ref[2]
    for role in range(4):
        d = 2 * jnp.bitwise_xor(me, role)
        for p in range(q_ref.shape[1]):
            even, odd = join(q_ref[d, p].astype(F32), q_ref[d + 1, p].astype(F32))
            out_ref[2 * p, :, role * 128 : (role + 1) * 128] = even.astype(BF16)
            out_ref[2 * p + 1, :, role * 128 : (role + 1) * 128] = odd.astype(BF16)


def attend_kernel(steps, first, last, pos_ref, q_ref, keep_ref, recv_ref, far_ref, *refs):
    count = sum(len(s) for s in steps)
    kv_refs, rest = refs[:count], refs[count:]
    me, yy = pos_ref[1] * 2 + pos_ref[2], pos_ref[4]
    acc = [None, None] if first else [rest[0][i] for i in range(2)]
    top = [None, None] if first else [rest[1][i, :1] for i in range(2)]
    at = 0
    for step in steps:
        bias = []
        for sh in step:
            y = lax.rem(yy + 8 + sh, 8)
            bias.append(
                jnp.concatenate([keep_ref[0, y], recv_ref[0, y], far_ref[0, y], far_ref[1, y]], axis=1).astype(F32)
            )
        bias = jnp.concatenate(bias, axis=0)
        blocks = kv_refs[at : at + len(step)]
        at += len(step)
        for i in range(2):
            keys = jnp.concatenate([jnp.transpose(r[i, :HD].astype(F32)).astype(BF16) for r in blocks], axis=0)
            vals = jnp.concatenate([r[i, HD:] for r in blocks], axis=1)
            vals = jnp.concatenate([vals, jnp.ones((16, vals.shape[1]), BF16)], axis=0)
            scores = jnp.dot(keys, q_ref[i], preferred_element_type=F32) + bias
            best = jnp.max(scores, axis=0, keepdims=True)
            if top[i] is not None:
                best = jnp.maximum(best, top[i])
            probs = jnp.exp(scores - best).astype(BF16)
            part = jnp.dot(vals, probs, preferred_element_type=F32)
            if top[i] is not None:
                part = part + acc[i] * jnp.exp(top[i] - best)
            acc[i], top[i] = part, best
    if not last:
        for i in range(2):
            rest[-2][i] = acc[i]
            rest[-1][i] = jnp.broadcast_to(top[i], (8, top[i].shape[1]))
        return
    out_ref = rest[-1]
    row = lax.broadcasted_iota(jnp.int32, (16, 128), 0)
    for role in range(4):
        d = 2 * jnp.bitwise_xor(me, role)
        tiles = []
        for i in range(2):
            mine = acc[i][:, role * 128 : (role + 1) * 128]
            total = mine[HD : HD + 1]
            lse = top[i][:, role * 128 : (role + 1) * 128] + jnp.log(total)
            hi = lse.astype(BF16).astype(F32)
            mid = (lse - hi).astype(BF16).astype(F32)
            low = lse - hi - mid
            tail = jnp.where(row == 0, hi, jnp.where(row == 1, mid, jnp.where(row == 2, low, 0.0)))
            tiles.append(jnp.concatenate([mine[:HD] / total, tail], axis=0))
        even, odd = join(tiles[0], tiles[1])
        out_ref[d, 0] = even.astype(BF16)
        out_ref[d + 1, 0] = odd.astype(BF16)


def merge_kernel(pos_ref, p_ref, gate_ref, out_ref):
    core = pos_ref[2]
    peers = out_ref.shape[0]
    tok = 64 // peers
    for p in range(p_ref.shape[1]):
        gated = []
        for other in range(2):
            h = jnp.bitwise_xor(core, other)
            rows = [p_ref[2 * i + h, p].astype(F32) for i in range(4)]
            lse = [r[HD : HD + 1] + r[HD + 1 : HD + 2] + r[HD + 2 : HD + 3] for r in rows]
            top = functools.reduce(jnp.maximum, lse)
            weight = [jnp.exp(v - top) for v in lse]
            gated.append(sum(w * r[:HD] for w, r in zip(weight, rows)) / sum(weight) * gate_ref[h, p])
        turned = jnp.transpose(jnp.concatenate(gated + [jnp.zeros((128 - 2 * HD, 128), F32)], axis=0))
        split = turned.reshape(2, peers, tok, 128)
        for g in range(peers):
            both = jnp.concatenate([split[0, g], split[1, g]], axis=0)
            out_ref[g, 2 * tok * p : 2 * tok * (p + 1)] = both.astype(BF16)


def out_kernel(g_ref, w_near_ref, w_far_ref, out_ref):
    total = None
    for g in range(g_ref.shape[0]):
        gated = g_ref[g]
        term = jnp.dot(gated[:, :HD], w_near_ref[g], preferred_element_type=F32)
        term = term + jnp.dot(gated[:, HD : 2 * HD], w_far_ref[g], preferred_element_type=F32)
        total = term if total is None else total + term
    out_ref[...] = total.astype(BF16)


def shift(x, axis, by):
    n = SIZES[AXES.index(axis)]
    return lax.ppermute(x, axis, [(i, (i + by) % n) for i in range(n)])


def body(tokens, chain_id, hotspots, chain_embed, hot_embed, w_proj, pair_bias, w_out):
    samples, tok_dev, width = tokens.shape
    pairs, peers = samples // 2, 8
    at = {a: lax.axis_index(a) for a in AXES}
    first = ((((at["y"] * 2 + at["xlo"]) * 2 + at["core"]) * 8 + at["z"]) * 2 + at["xhi"]) * tok_dev
    pos = jnp.stack([first, at["xlo"], at["core"], at["xhi"], at["y"]])
    vm = pl.BlockSpec(memory_space=pltpu.VMEM)
    sm = pl.BlockSpec(memory_space=pltpu.SMEM)

    def call(kernel, specs, out, *args, scratch=(), mib=16):
        shapes = [jax.ShapeDtypeStruct(s, t) for s, t in out]
        return pl.pallas_call(
            kernel,
            out_shape=shapes,
            in_specs=specs,
            out_specs=[vm] * len(out),
            scratch_shapes=scratch,
            compiler_params=params(mib),
        )(*args)

    def exchange(x, axes):
        return lax.all_to_all(x, axes, split_axis=0, concat_axis=0, tiled=True)

    weights = jnp.concatenate([jnp.transpose(w_proj), w_out], axis=0)
    weights_other = shift(weights, "xhi", 1)
    keep, away = call(
        bias_kernel,
        [sm, vm],
        [((2, 8, 128, 128), BF16)] * 2,
        pos,
        pair_bias,
        scratch=[pltpu.VMEM((32, 128, 128), BF16)],
    )
    recv = shift(away, "core", 1)
    far_out = jnp.stack([keep[1], recv[1]])

    (copies,) = call(
        norm_kernel,
        [sm, sm, sm, vm, vm, vm],
        [((peers, samples * tok_dev, width), BF16)],
        first[None],
        chain_id,
        hotspots,
        tokens,
        chain_embed,
        hot_embed,
        mib=56,
    )
    gathered = exchange(copies, "z")
    weights_other, far_out = lax.optimization_barrier((weights_other, far_out))
    far = shift(far_out, "xlo", 1)
    gathered, far_out = lax.optimization_barrier((gathered, far_out))
    q_out, kv_own, kv_other, gate, w_copies = call(
        proj_kernel,
        [sm, vm, vm, vm],
        [
            ((8, pairs, HD, 128), BF16),
            ((pairs, 2 * HD, 128), BF16),
            ((pairs, 2 * HD, 128), BF16),
            ((2, pairs, HD, 128), F32),
            ((peers, HD, width), BF16),
        ],
        pos,
        gathered,
        weights,
        weights_other,
    )
    w_near = exchange(w_copies, "z")
    kv_other = shift(kv_other, "xhi", 1)
    (kv,) = call(join_kernel, [vm, vm], [((samples, 2 * HD, 128), BF16)], kv_own, kv_other)

    right, left, ring, shifts = kv, kv, [kv], [0]
    for step in range(1, 5):
        right = shift(right, "y", 1)
        ring.append(right)
        shifts.append(-step)
        if step < 4:
            left = shift(left, "y", -1)
            if step == 1:
                left, q_out, w_near = lax.optimization_barrier((left, q_out, w_near))
            ring.append(left)
            shifts.append(step)
    q_in = exchange(q_out, OCT)
    (q_all,) = call(join_q_kernel, [sm, vm], [((samples, HD, 512), BF16)], pos, q_in)

    def two(*dims):
        return pl.BlockSpec((2,) + dims, lambda s, _: (s,) + (0,) * len(dims))

    whole = pl.BlockSpec((2, 8, 128, 128), lambda s, _: (0, 0, 0, 0))
    state = (((samples, 64, 512), F32), ((samples, 8, 512), F32))

    def attend(blocks, carried, last):
        out = [((8, pairs, 64, 128), BF16)] if last else state
        state_specs = [two(64, 512), two(8, 512)]
        return pl.pallas_call(
            functools.partial(attend_kernel, (tuple(shifts[i] for i in blocks),), not carried, last),
            out_shape=[jax.ShapeDtypeStruct(s, t) for s, t in out],
            grid_spec=pltpu.PrefetchScalarGridSpec(
                num_scalar_prefetch=1,
                grid=(pairs,),
                in_specs=[two(HD, 512), whole, whole, whole]
                + [two(2 * HD, 128)] * len(blocks)
                + (state_specs if carried else []),
                out_specs=[pl.BlockSpec((8, 1, 64, 128), lambda s, _: (0, s, 0, 0))] if last else state_specs,
            ),
            compiler_params=params(24),
            cost_estimate=pl.CostEstimate(
                flops=len(blocks) << 30, bytes_accessed=4 << 20, transcendentals=len(blocks) << 19
            ),
        )(pos, q_all, keep, recv, far, *[ring[i] for i in blocks], *carried)

    carried = attend((0, 1, 2, 3, 4, 5), [], False)
    (parts,) = attend((6, 7), carried, True)
    parts, w_near = lax.optimization_barrier((parts, w_near))
    w_far = shift(w_near, "core", 1)
    mine = exchange(parts, OCT)
    (gated,) = call(
        merge_kernel, [sm, vm, vm], [((peers, samples * tok_dev, 128), BF16)], pos, mine, gate
    )
    (update,) = call(
        out_kernel, [vm, vm, vm], [((samples * tok_dev, width), BF16)], exchange(gated, "z"), w_near, w_far
    )
    return update.reshape(samples, tok_dev, width)


def solution(mesh):
    fine = Mesh(np.asarray(mesh.devices).reshape(SIZES), AXES)
    blk = ("y", "xlo", "core")
    in_specs = (
        P(None, AXES, None),
        P(AXES),
        P(),
        P(),
        P(),
        P(None, HEADS),
        P(HEADS, blk, None),
        P(HEADS, None),
    )
    return jax.shard_map(body, mesh=fine, in_specs=in_specs, out_specs=P(None, AXES, None), check_vma=False)
```

```python
import functools

import jax
import jax.numpy as jnp
import numpy as np
from jax import lax
from jax.experimental import pallas as pl
from jax.experimental.pallas import tpu as pltpu
from jax.sharding import Mesh
from jax.sharding import PartitionSpec as P

HD = 48
AXES = ("y", "xlo", "core", "z", "xhi")
SIZES = (8, 2, 2, 8, 2)
HEADS = ("z", "xhi")
OCT = ("xlo", "core", "xhi")
F32, BF16 = jnp.float32, jnp.bfloat16
MIB = 1024 * 1024


def params(mib=16):
    return pltpu.CompilerParams(vmem_limit_bytes=mib * MIB)


def dot(a, b, da, db):
    return lax.dot_general(a, b, (((da,), (db,)), ((), ())), preferred_element_type=F32)


def norm_kernel(pos_ref, chain_ref, hot_ref, tok_ref, emb_ref, hemb_ref, out_ref):
    samples, tok_dev, width = tok_ref.shape
    first = pos_ref[0]
    emb = emb_ref[...].astype(F32)
    hemb = hemb_ref[...].astype(F32).reshape(1, width)
    row_of = lax.broadcasted_iota(jnp.int32, (tok_dev, width), 0)
    cond = jnp.zeros((tok_dev, width), F32)
    for t in range(tok_dev):
        chain = chain_ref[t]
        row = jnp.zeros((1, width), F32)
        for c in range(emb_ref.shape[0]):
            row = row + jnp.where(chain == c, 1.0, 0.0) * emb[c : c + 1]
        hits = jnp.int32(0)
        for i in range(hot_ref.shape[0]):
            hits = hits + jnp.where(hot_ref[i] == first + t, 1, 0)
        row = row + jnp.where(hits > 0, 1.0, 0.0) * hemb
        cond = cond + jnp.where(row_of == t, row, 0.0)
    shifted = tok_ref[...].astype(F32) + cond[None]
    average = jnp.mean(shifted, axis=-1, keepdims=True)
    centred = shifted - average
    spread = jnp.mean(centred * centred, axis=-1, keepdims=True)
    normed = (centred * lax.rsqrt(spread + 1e-05)).reshape(samples * tok_dev, width).astype(BF16)
    for g in range(out_ref.shape[0]):
        out_ref[g] = normed


def bias_kernel(pos_ref, b_ref, keep_ref, away_ref, rows_ref):
    xlo, core, xhi = pos_ref[1], pos_ref[2], pos_ref[3]
    row = lax.broadcasted_iota(jnp.int32, (128, 128), 0)
    col = lax.broadcasted_iota(jnp.int32, (128, 128), 1)
    z, t = (row % 64) // 8, row % 8
    from_q = (z * 2 + row // 64) * 8 + t
    from_k = (z * 2 + jnp.bitwise_xor(row // 64, xhi)) * 8 + t
    pick_q = jnp.where(col == from_q, 1.0, 0.0).astype(BF16)
    pick_k = jnp.where(col == from_k, 1.0, 0.0).astype(BF16)
    for b in range(32):
        rows_ref[b] = dot(pick_q, b_ref[0, :, b * 128 : (b + 1) * 128], 1, 0).astype(BF16)
    for role in range(2):
        xl = jnp.bitwise_xor(xlo, role)
        for y in range(8):
            at = (y * 2 + xl) * 2
            keep_ref[role, y] = dot(pick_k, rows_ref[at + core], 1, 1).astype(BF16)
            away_ref[role, y] = dot(pick_k, rows_ref[at + 1 - core], 1, 1).astype(BF16)


def proj_kernel(pos_ref, x_ref, own_ref, other_ref, q_ref, kv_own_ref, kv_other_ref, gate_ref, w_ref):
    peers, rows, width = x_ref.shape
    pairs = kv_own_ref.shape[0]
    tok = rows // (2 * pairs)
    xhi = pos_ref[3]
    x = x_ref[...].reshape(peers * rows, width)
    for role, in_ref in enumerate((own_ref, other_ref)):
        kv_ref = (kv_own_ref, kv_other_ref)[role]

        @pl.when(jnp.bitwise_xor(pos_ref[2], xhi) == role)
        def _():
            for g in range(peers):
                w_ref[g] = in_ref[4 * HD :]

        full = dot(x, in_ref[: 4 * HD], 1, 1).reshape(peers, 2 * pairs, tok, 4 * HD)
        for p in range(pairs):
            two = jnp.concatenate([full[:, 2 * p + i].reshape(peers * tok, 4 * HD) for i in range(2)], axis=0)
            turned = jnp.transpose(two)
            queries = (turned[:HD] * (1.0 / HD**0.5)).astype(BF16)
            for d in range(4):
                q_ref[2 * d + jnp.bitwise_xor(xhi, role), p] = queries
            kv_ref[p] = turned[HD : 3 * HD].astype(BF16)
            gate_ref[jnp.bitwise_xor(xhi, role), p] = jax.nn.sigmoid(turned[3 * HD :])


def join(a, b):
    lane = lax.broadcasted_iota(jnp.int32, a.shape, 1)
    return jnp.where(lane < 64, a, pltpu.roll(b, 64, 1)), jnp.where(lane < 64, pltpu.roll(a, 64, 1), b)


def join_kernel(own_ref, other_ref, kv_ref):
    for p in range(own_ref.shape[0]):
        even, odd = join(own_ref[p].astype(F32), other_ref[p].astype(F32))
        kv_ref[2 * p] = even.astype(BF16)
        kv_ref[2 * p + 1] = odd.astype(BF16)


def join_q_kernel(pos_ref, q_ref, out_ref):
    me = pos_ref[1] * 2 + pos_ref[2]
    for role in range(4):
        d = 2 * jnp.bitwise_xor(me, role)
        for p in range(q_ref.shape[1]):
            even, odd = join(q_ref[d, p].astype(F32), q_ref[d + 1, p].astype(F32))
            out_ref[2 * p, :, role * 128 : (role + 1) * 128] = even.astype(BF16)
            out_ref[2 * p + 1, :, role * 128 : (role + 1) * 128] = odd.astype(BF16)


def attend_kernel(steps, first, last, pos_ref, q_ref, keep_ref, recv_ref, far_ref, *refs):
    count = sum(len(s) for s in steps)
    kv_refs, rest = refs[:count], refs[count:]
    me, yy = pos_ref[1] * 2 + pos_ref[2], pos_ref[4]
    acc = [None, None] if first else [rest[0][i] for i in range(2)]
    top = [None, None] if first else [rest[1][i, :1] for i in range(2)]
    at = 0
    for step in steps:
        bias = []
        for sh in step:
            y = lax.rem(yy + 8 + sh, 8)
            bias.append(
                jnp.concatenate([keep_ref[0, y], recv_ref[0, y], far_ref[0, y], far_ref[1, y]], axis=1).astype(F32)
            )
        bias = jnp.concatenate(bias, axis=0)
        blocks = kv_refs[at : at + len(step)]
        at += len(step)
        for i in range(2):
            keys = jnp.concatenate([jnp.transpose(r[i, :HD].astype(F32)).astype(BF16) for r in blocks], axis=0)
            vals = jnp.concatenate([r[i, HD:] for r in blocks], axis=1)
            vals = jnp.concatenate([vals, jnp.ones((16, vals.shape[1]), BF16)], axis=0)
            scores = jnp.dot(keys, q_ref[i], preferred_element_type=F32) + bias
            best = jnp.max(scores, axis=0, keepdims=True)
            if top[i] is not None:
                best = jnp.maximum(best, top[i])
            probs = jnp.exp(scores - best).astype(BF16)
            part = jnp.dot(vals, probs, preferred_element_type=F32)
            if top[i] is not None:
                part = part + acc[i] * jnp.exp(top[i] - best)
            acc[i], top[i] = part, best
    if not last:
        for i in range(2):
            rest[-2][i] = acc[i]
            rest[-1][i] = jnp.broadcast_to(top[i], (8, top[i].shape[1]))
        return
    out_ref = rest[-1]
    row = lax.broadcasted_iota(jnp.int32, (16, 128), 0)
    for role in range(4):
        d = 2 * jnp.bitwise_xor(me, role)
        tiles = []
        for i in range(2):
            mine = acc[i][:, role * 128 : (role + 1) * 128]
            total = mine[HD : HD + 1]
            lse = top[i][:, role * 128 : (role + 1) * 128] + jnp.log(total)
            hi = lse.astype(BF16).astype(F32)
            mid = (lse - hi).astype(BF16).astype(F32)
            low = lse - hi - mid
            tail = jnp.where(row == 0, hi, jnp.where(row == 1, mid, jnp.where(row == 2, low, 0.0)))
            tiles.append(jnp.concatenate([mine[:HD] / total, tail], axis=0))
        even, odd = join(tiles[0], tiles[1])
        out_ref[d, 0] = even.astype(BF16)
        out_ref[d + 1, 0] = odd.astype(BF16)


def merge_kernel(pos_ref, p_ref, gate_ref, out_ref):
    core = pos_ref[2]
    peers = out_ref.shape[0]
    tok = 64 // peers
    for p in range(p_ref.shape[1]):
        gated = []
        for other in range(2):
            h = jnp.bitwise_xor(core, other)
            rows = [p_ref[2 * i + h, p].astype(F32) for i in range(4)]
            lse = [r[HD : HD + 1] + r[HD + 1 : HD + 2] + r[HD + 2 : HD + 3] for r in rows]
            top = functools.reduce(jnp.maximum, lse)
            weight = [jnp.exp(v - top) for v in lse]
            gated.append(sum(w * r[:HD] for w, r in zip(weight, rows)) / sum(weight) * gate_ref[h, p])
        turned = jnp.transpose(jnp.concatenate(gated + [jnp.zeros((128 - 2 * HD, 128), F32)], axis=0))
        split = turned.reshape(2, peers, tok, 128)
        for g in range(peers):
            both = jnp.concatenate([split[0, g], split[1, g]], axis=0)
            out_ref[g, 2 * tok * p : 2 * tok * (p + 1)] = both.astype(BF16)


def out_kernel(g_ref, w_near_ref, w_far_ref, out_ref):
    total = None
    for g in range(g_ref.shape[0]):
        gated = g_ref[g]
        term = jnp.dot(gated[:, :HD], w_near_ref[g], preferred_element_type=F32)
        term = term + jnp.dot(gated[:, HD : 2 * HD], w_far_ref[g], preferred_element_type=F32)
        total = term if total is None else total + term
    out_ref[...] = total.astype(BF16)


def shift(x, axis, by):
    n = SIZES[AXES.index(axis)]
    return lax.ppermute(x, axis, [(i, (i + by) % n) for i in range(n)])


def body(tokens, chain_id, hotspots, chain_embed, hot_embed, w_proj, pair_bias, w_out):
    samples, tok_dev, width = tokens.shape
    pairs, peers = samples // 2, 8
    at = {a: lax.axis_index(a) for a in AXES}
    first = ((((at["y"] * 2 + at["xlo"]) * 2 + at["core"]) * 8 + at["z"]) * 2 + at["xhi"]) * tok_dev
    pos = jnp.stack([first, at["xlo"], at["core"], at["xhi"], at["y"]])
    vm = pl.BlockSpec(memory_space=pltpu.VMEM)
    sm = pl.BlockSpec(memory_space=pltpu.SMEM)

    def call(kernel, specs, out, *args, scratch=(), mib=16):
        shapes = [jax.ShapeDtypeStruct(s, t) for s, t in out]
        return pl.pallas_call(
            kernel,
            out_shape=shapes,
            in_specs=specs,
            out_specs=[vm] * len(out),
            scratch_shapes=scratch,
            compiler_params=params(mib),
        )(*args)

    def exchange(x, axes):
        return lax.all_to_all(x, axes, split_axis=0, concat_axis=0, tiled=True)

    weights = jnp.concatenate([jnp.transpose(w_proj), w_out], axis=0)
    weights_other = shift(weights, "xhi", 1)
    keep, away = call(
        bias_kernel,
        [sm, vm],
        [((2, 8, 128, 128), BF16)] * 2,
        pos,
        pair_bias,
        scratch=[pltpu.VMEM((32, 128, 128), BF16)],
    )
    recv = shift(away, "core", 1)
    far_out = jnp.stack([keep[1], recv[1]])

    (copies,) = call(
        norm_kernel,
        [sm, sm, sm, vm, vm, vm],
        [((peers, samples * tok_dev, width), BF16)],
        first[None],
        chain_id,
        hotspots,
        tokens,
        chain_embed,
        hot_embed,
        mib=56,
    )
    gathered = exchange(copies, "z")
    weights_other, far_out = lax.optimization_barrier((weights_other, far_out))
    far = shift(far_out, "xlo", 1)
    gathered, far_out = lax.optimization_barrier((gathered, far_out))
    q_out, kv_own, kv_other, gate, w_copies = call(
        proj_kernel,
        [sm, vm, vm, vm],
        [
            ((8, pairs, HD, 128), BF16),
            ((pairs, 2 * HD, 128), BF16),
            ((pairs, 2 * HD, 128), BF16),
            ((2, pairs, HD, 128), F32),
            ((peers, HD, width), BF16),
        ],
        pos,
        gathered,
        weights,
        weights_other,
    )
    kv_other = shift(kv_other, "xhi", 1)
    (kv,) = call(join_kernel, [vm, vm], [((samples, 2 * HD, 128), BF16)], kv_own, kv_other)

    right, left, ring, shifts = kv, kv, [kv], [0]
    for step in range(1, 5):
        right = shift(right, "y", 1)
        ring.append(right)
        shifts.append(-step)
        if step < 4:
            left = shift(left, "y", -1)
            if step == 1:
                left, q_out = lax.optimization_barrier((left, q_out))
            ring.append(left)
            shifts.append(step)
    q_in = exchange(q_out, OCT)
    w_copies, q_in = lax.optimization_barrier((w_copies, q_in))
    w_near = exchange(w_copies, "z")
    (q_all,) = call(join_q_kernel, [sm, vm], [((samples, HD, 512), BF16)], pos, q_in)

    def two(*dims):
        return pl.BlockSpec((2,) + dims, lambda s, _: (s,) + (0,) * len(dims))

    whole = pl.BlockSpec((2, 8, 128, 128), lambda s, _: (0, 0, 0, 0))
    state = (((samples, 64, 512), F32), ((samples, 8, 512), F32))

    def attend(blocks, carried, last):
        out = [((8, pairs, 64, 128), BF16)] if last else state
        state_specs = [two(64, 512), two(8, 512)]
        return pl.pallas_call(
            functools.partial(attend_kernel, (tuple(shifts[i] for i in blocks),), not carried, last),
            out_shape=[jax.ShapeDtypeStruct(s, t) for s, t in out],
            grid_spec=pltpu.PrefetchScalarGridSpec(
                num_scalar_prefetch=1,
                grid=(pairs,),
                in_specs=[two(HD, 512), whole, whole, whole]
                + [two(2 * HD, 128)] * len(blocks)
                + (state_specs if carried else []),
                out_specs=[pl.BlockSpec((8, 1, 64, 128), lambda s, _: (0, s, 0, 0))] if last else state_specs,
            ),
            compiler_params=params(24),
            cost_estimate=pl.CostEstimate(
                flops=len(blocks) << 30, bytes_accessed=4 << 20, transcendentals=len(blocks) << 19
            ),
        )(pos, q_all, keep, recv, far, *[ring[i] for i in blocks], *carried)

    carried = attend((0, 1, 2, 3, 4, 5), [], False)
    (parts,) = attend((6, 7), carried, True)
    parts, w_near = lax.optimization_barrier((parts, w_near))
    w_far = shift(w_near, "core", 1)
    mine = exchange(parts, OCT)
    (gated,) = call(
        merge_kernel, [sm, vm, vm], [((peers, samples * tok_dev, 128), BF16)], pos, mine, gate
    )
    (update,) = call(
        out_kernel, [vm, vm, vm], [((samples * tok_dev, width), BF16)], exchange(gated, "z"), w_near, w_far
    )
    return update.reshape(samples, tok_dev, width)


def solution(mesh):
    fine = Mesh(np.asarray(mesh.devices).reshape(SIZES), AXES)
    blk = ("y", "xlo", "core")
    in_specs = (
        P(None, AXES, None),
        P(AXES),
        P(),
        P(),
        P(),
        P(None, HEADS),
        P(HEADS, blk, None),
        P(HEADS, None),
    )
    return jax.shard_map(body, mesh=fine, in_specs=in_specs, out_specs=P(None, AXES, None), check_vma=False)
```
